32 devices in a mesh: section: 2 (over y), expert: 16 (over z, x, core).
Axes of the slice: x: 2, y: 2, z: 4, core: 2. Of those that a mesh axis runs over, the one named last changes fastest.
Arguments:
- tokens: bfloat16 [2, 128, 3584], P('section', 'expert'), may hold values from -6 to 6
- norm_gain: bfloat16 [2, 3584], P('section'), may hold values from 0.5 to 1.5
- router: bfloat16 [2, 3584, 16], P('section'), may hold values from -0.09375 to 0.09375
- w_gate: bfloat16 [2, 16, 3584, 1024], P('section', 'expert'), may hold values from -0.09375 to 0.09375
- w_up: bfloat16 [2, 16, 3584, 1024], P('section', 'expert'), may hold values from -0.09375 to 0.09375
- w_down: bfloat16 [2, 16, 1024, 3584], P('section', 'expert'), may hold values from -0.1875 to 0.1875
- expert_ids: int32 [2, 2, 128, 8], P('section', None, 'expert'), may hold values from 0 to 15, all different within a row
Outputs:
- mixed: bfloat16 [2, 128, 3584], P('section', 'expert')
The draws below stay inside these ranges and needn't reach their ends.
Inputs may be any that keep to these rules, and one draw needn't show every extreme that they name: `expert_ids`: each row names 8 different experts.
All inputs are finite; a program needn't handle non-finite values.
Results may differ from the reference program's by a relative error of at most 0.022.
Values may be sent and summed in bfloat16 or wider, within the bound.
No kernel may reach another device: no remote copies, remote signals or barrier semaphores. Data moves between devices by JAX's collectives and lax.ppermute only.
A program may use at most 128 MiB of HBM per device.

```python
import jax
import jax.numpy as jnp
from jax import lax

D = 3584
FF = 1024
TOPK = 8
TOK_DEV = 8
EXPERTS = 16
LAYERS = 2
MICRO = 2
TOKENS = 128
CAP = 5
N_EXPERT = 16


def shard_levels(rng, shape, cuts, smallest, high):
    factor_of, own = 1.0, jax.random.fold_in(rng, 6)
    for dim, blocks in cuts:
        heights = jnp.exp(jax.random.uniform(jax.random.fold_in(own, dim), (blocks,), jnp.float32, smallest / len(cuts), high / len(cuts)))
        factor_of = factor_of * jnp.repeat(heights, shape[dim] // blocks).reshape([-1 if axis == dim else 1 for axis in range(len(shape))])
    return factor_of


def picks_of(rng, rows, number_of, top, lift):
    order = jax.random.permutation(jax.random.fold_in(rng, 1), number_of)
    pull = order
    for power in range(3):
        pull = pull * pull // number_of
    pull = pull * lift // number_of
    tickets = jax.random.randint(jax.random.fold_in(rng, 2), (rows, number_of), 0, 4096) + pull
    holders = jax.random.permutation(jax.random.fold_in(rng, 3), rows)[jnp.arange(number_of) % rows]
    tickets = jnp.where(jnp.arange(rows)[:, None] == holders[None, :], 1 << 14, tickets)
    priority = tickets * number_of + jnp.arange(number_of)
    return lax.top_k(priority.astype(jnp.int32), top)[1].astype(jnp.int32)


def centred(rng, extent, width, most, split=(), kind=jnp.bfloat16):
    loudness = shard_levels(rng, extent, split, -0.22, 0.18) if split else 1.0
    values = jax.random.normal(rng, extent, jnp.float32) * width * loudness
    return jnp.minimum(jnp.maximum(values, -most), most).astype(kind)


def setup_inputs(seed: int = 0) -> dict:
    splits = jax.random.split(jax.random.key(seed), 8)
    tokens = centred(splits[0], (MICRO, TOKENS, D), 1.0, 6.0, ((0, 2), (1, 16)))
    norm_gain = jnp.clip(1.0 + 0.1 * jax.random.normal(splits[1], (LAYERS, D), jnp.float32), 0.5, 1.5).astype(jnp.bfloat16)
    router = centred(splits[2], (LAYERS, D, EXPERTS), D ** -0.5, 0.09375, ((0, 2),))
    w_gate = centred(splits[3], (LAYERS, EXPERTS, D, FF), D ** -0.5, 0.09375, ((0, 2), (1, 16)))
    w_up = centred(splits[4], (LAYERS, EXPERTS, D, FF), D ** -0.5, 0.09375, ((0, 2), (1, 16)))
    w_down = centred(splits[5], (LAYERS, EXPERTS, FF, D), FF ** -0.5, 0.1875, ((0, 2), (1, 16)))
    expert_ids = picks_of(splits[6], LAYERS * MICRO * TOKENS, EXPERTS, TOPK, 8192).reshape((LAYERS, MICRO, TOKENS, TOPK))
    return {"tokens": tokens, "norm_gain": norm_gain, "router": router, "w_gate": w_gate, "w_up": w_up, "w_down": w_down, "expert_ids": expert_ids}


epsilon = 1e-06
routed_scale = 2.5

def normalize(hidden_rows, gain_row):
    values = hidden_rows.astype(jnp.float32)
    inverse_rms = lax.rsqrt(lax.optimization_barrier(jnp.mean(values * values, axis=-1, keepdims=True)) + epsilon)
    return (values * inverse_rms * gain_row.astype(jnp.float32)).astype(jnp.bfloat16)

def route(normed, choices, router_cols, blocks):
    expert_count = router_cols.shape[1]
    logits = jnp.dot(normed, router_cols, preferred_element_type=jnp.float32)
    scores = jax.nn.sigmoid(logits)
    onehot = choices[:, :, None] == jnp.arange(expert_count, dtype=jnp.int32)[None, None, :]
    picked = lax.optimization_barrier(jnp.sum(jnp.where(onehot, scores[:, None, :], 0.0), axis=-1))
    weights = routed_scale * picked / lax.optimization_barrier(jnp.sum(picked, axis=-1, keepdims=True))
    indicator = onehot.astype(jnp.int32).reshape(blocks, -1, expert_count)
    earlier = jnp.cumsum(indicator, axis=1) - indicator
    positions = lax.optimization_barrier(jnp.sum(earlier * indicator, axis=-1)).reshape(choices.shape)
    return (weights, positions.astype(jnp.int32))

def expert_mlp(inputs, gate_weight, up_weight, down_weight):
    gate_part = jnp.dot(inputs, gate_weight, preferred_element_type=jnp.float32)
    up_part = jnp.dot(inputs, up_weight, preferred_element_type=jnp.float32)
    hidden = (jax.nn.silu(gate_part) * up_part).astype(jnp.bfloat16)
    return jnp.dot(hidden, down_weight, preferred_element_type=jnp.float32).astype(jnp.bfloat16)

def moe_layer(hidden_rows, gain_row, router_cols, gate_all, up_all, down_all, choices):
    normed = normalize(hidden_rows, gain_row)
    weights, positions = route(normed, choices, router_cols, N_EXPERT)
    retained = positions < CAP
    source_block = (jnp.arange(TOKENS, dtype=jnp.int32) // TOK_DEV)[:, None]
    slot_keys = (choices * (N_EXPERT * CAP) + source_block * CAP + positions).astype(jnp.int32)
    total_slots = EXPERTS * N_EXPERT * CAP
    target = jnp.where(retained, slot_keys, total_slots).astype(jnp.int32)
    buffer = jnp.zeros((total_slots, D), jnp.bfloat16).at[target.reshape(-1)].set(jnp.repeat(normed, TOPK, axis=0), mode='drop')

    def serve_expert(operands):
        rows_in, gate_weight, up_weight, down_weight = operands
        return expert_mlp(rows_in, gate_weight, up_weight, down_weight)
    produced = lax.map(serve_expert, (buffer.reshape(EXPERTS, N_EXPERT * CAP, D), gate_all, up_all, down_all))
    flattened = produced.reshape(total_slots, D)
    picked = flattened[jnp.where(retained, slot_keys, 0).astype(jnp.int32)]
    factor = jnp.where(retained, weights, 0.0)
    branch = jnp.einsum('tk,tkd->td', factor, picked.astype(jnp.float32))
    return (hidden_rows.astype(jnp.float32) + branch).astype(jnp.bfloat16)

def reference(tokens, norm_gain, router, w_gate, w_up, w_down, expert_ids):
    outputs = []
    for micro_index in range(MICRO):
        hidden_rows = tokens[micro_index]
        for layer_index in range(LAYERS):
            hidden_rows = moe_layer(hidden_rows, norm_gain[layer_index], router[layer_index], w_gate[layer_index], w_up[layer_index], w_down[layer_index], expert_ids[layer_index, micro_index])
        outputs.append(hidden_rows)
    return jnp.stack(outputs)
```

```python
import jax
import jax.numpy as jnp
from jax import lax
from jax.sharding import PartitionSpec as P

epsilon = 1e-06
routed_scale = 2.5
everywhere = ("section", "expert")


def normalize(hidden_rows, gain_row):
    values = hidden_rows.astype(jnp.float32)
    inverse_rms = lax.rsqrt(jnp.mean(values * values, axis=-1, keepdims=True) + epsilon)
    return (values * inverse_rms * gain_row.astype(jnp.float32)).astype(jnp.bfloat16)


def member_table(choices, expert_count):
    names = jnp.arange(expert_count, dtype=jnp.int32)
    return jnp.any(choices[:, :, None] == names[None, None, :], axis=1)


def kept_rows(member, owner_index, row_count, capacity):
    mine = jnp.arange(member.shape[1], dtype=jnp.int32) == owner_index
    named = jnp.any(member & mine[None, :], axis=1).reshape(-1, row_count)
    counted = named.astype(jnp.int32)
    earlier = jnp.cumsum(counted, axis=1) - counted
    return (named & (earlier < capacity)).reshape(-1)


def own_weights(normed, router_cols, member, owner_index):
    logits = jnp.dot(normed, router_cols, preferred_element_type=jnp.float32)
    scores = jax.nn.sigmoid(logits)
    mine = jnp.arange(member.shape[1], dtype=jnp.int32) == owner_index
    total = jnp.sum(jnp.where(member, scores, 0.0), axis=-1)
    own = jnp.sum(jnp.where(mine[None, :], scores, 0.0), axis=-1)
    return routed_scale * own / total


def expert_mlp(inputs, gate_weight, up_weight, down_weight):
    gate_part = jnp.dot(inputs, gate_weight, preferred_element_type=jnp.float32)
    up_part = jnp.dot(inputs, up_weight, preferred_element_type=jnp.float32)
    hidden = (jax.nn.silu(gate_part) * up_part).astype(jnp.bfloat16)
    return jnp.dot(hidden, down_weight, preferred_element_type=jnp.float32)


def per_device(tokens, norm_gain, router, w_gate, w_up, w_down, expert_ids):
    sections = lax.axis_size("section")
    section_index = lax.axis_index("section")
    expert_count = lax.axis_size("expert")
    owner_index = lax.axis_index("expert")
    micro_count = expert_ids.shape[1]
    row_count = tokens.shape[1]
    model_width = tokens.shape[2]
    top_count = expert_ids.shape[3]
    capacity = min(row_count, max(2, 5 * row_count * top_count // (4 * expert_count)))

    named = jnp.transpose(expert_ids[0], (1, 0, 2)).reshape(row_count, -1)
    pad = -named.shape[1] % 128
    named = jnp.pad(named.astype(jnp.bfloat16), ((0, 0), (0, pad)))
    packed = jnp.concatenate([tokens[0], named], axis=1)
    gathered = lax.all_gather(packed, everywhere, axis=0, tiled=True)
    hidden_rows = gathered[:, :model_width]
    choices = gathered[:, model_width : model_width + micro_count * top_count]
    choices = choices.reshape(sections, expert_count, row_count, micro_count, top_count)
    choices = lax.dynamic_index_in_dim(choices, section_index, 0, keepdims=False)
    choices = jnp.transpose(choices, (2, 0, 1, 3)).reshape(-1, top_count).astype(jnp.int32)

    member = member_table(choices, expert_count)
    kept = kept_rows(member, owner_index, row_count, capacity)
    for layer in range(sections):
        normed = normalize(hidden_rows, norm_gain[0])
        weights = own_weights(normed, router[0], member, owner_index)
        factor = jnp.where(kept & (section_index == layer), weights, 0.0)
        produced = expert_mlp(normed, w_gate[0, 0], w_up[0, 0], w_down[0, 0])
        share = (produced * factor[:, None]).astype(jnp.bfloat16)
        if layer < sections - 1:
            branch = lax.psum(share, everywhere)
            hidden_rows = (hidden_rows.astype(jnp.float32) + branch.astype(jnp.float32)).astype(jnp.bfloat16)
    branch = lax.psum_scatter(share, everywhere, scatter_dimension=0, tiled=True)
    first = (section_index * expert_count + owner_index) * row_count
    own_rows = lax.dynamic_slice_in_dim(hidden_rows, first, row_count, 0)
    mixed = (own_rows.astype(jnp.float32) + branch.astype(jnp.float32)).astype(jnp.bfloat16)
    return mixed[None]


def solution(mesh):
    placed = (
        P("section", "expert", None),
        P("section", None),
        P("section", None, None),
        P("section", "expert", None, None),
        P("section", "expert", None, None),
        P("section", "expert", None, None),
        P("section", None, "expert", None),
    )
    return jax.shard_map(
        per_device,
        mesh=mesh,
        in_specs=placed,
        out_specs=P("section", "expert", None),
        check_vma=False,
    )
```

```python
import functools

import jax
import jax.numpy as jnp
from jax import lax
from jax.experimental import pallas as pl
from jax.experimental.pallas import tpu as pltpu
from jax.sharding import PartitionSpec as P

epsilon = 1e-06
routed_scale = 2.5
lanes = 128
inner_size = 4


def norm_kernel(hidden_ref, gain_ref, *rest):
    *ids_ref, out_ref = rest
    row_count, width = hidden_ref.shape
    values = hidden_ref[...].astype(jnp.float32)
    inverse_rms = lax.rsqrt(jnp.mean(values * values, axis=-1, keepdims=True) + epsilon)
    normed = (values * inverse_rms * gain_ref[...].astype(jnp.float32)).astype(jnp.bfloat16)
    if ids_ref:
        micro_count, _, top_count = ids_ref[0].shape
        lane_at = lax.broadcasted_iota(jnp.int32, (row_count, lanes), 1)
        named = jnp.zeros((row_count, lanes), jnp.float32)
        for m in range(micro_count):
            choices = ids_ref[0][m].astype(jnp.float32)
            for k in range(top_count):
                named = jnp.where(lane_at == m * top_count + k, choices[:, k : k + 1], named)
        normed = jnp.concatenate([normed, named.astype(jnp.bfloat16)], axis=1)
    out_ref[...] = normed


def normalize(hidden_rows, gain_rows, *ids):
    row_count, width = hidden_rows.shape
    in_vmem = pl.BlockSpec(memory_space=pltpu.VMEM)
    return pl.pallas_call(
        norm_kernel,
        out_shape=jax.ShapeDtypeStruct((row_count, width + lanes * len(ids)), jnp.bfloat16),
        in_specs=[in_vmem] * (2 + len(ids)),
        out_specs=in_vmem,
        compiler_params=pltpu.CompilerParams(vmem_limit_bytes=4 * 1024 * 1024),
    )(hidden_rows, gain_rows, *ids)


def gather_rows(rows):
    inner = inner_size
    outer = lax.axis_size("expert") // inner
    same_place = [[o * inner + i for o in range(outer)] for i in range(inner)]
    same_group = [[o * inner + i for i in range(inner)] for o in range(outer)]
    rows = lax.all_gather(rows, "expert", axis=0, tiled=True, axis_index_groups=same_place)
    return lax.all_gather(rows, "expert", axis=0, tiled=True, axis_index_groups=same_group)


def expert_kernel(
    micro_index, top_count, row_count, capacity, outer,
    owner_ref, rows_ref, ids_ref, router_ref, gate_hbm, up_hbm, down_hbm, out_ref,
    gate_ref, up_ref, down_ref, hidden_ref, sems,
):
    total_rows, width = out_ref.shape
    expert_count = router_ref.shape[0]
    inner_width = gate_hbm.shape[1]
    inner_step, outer_step = 256, 512
    pieces = [
        (source, target, at, inner_step)
        for at in range(0, inner_width, inner_step)
        for source, target in ((gate_hbm, gate_ref), (up_hbm, up_ref))
    ]
    pieces += [(down_hbm, down_ref, at, outer_step) for at in range(0, width, outer_step)]
    copies = []
    for i, (source, target, at, step) in enumerate(pieces):
        part = (slice(None), pl.ds(at, step))
        copies.append(pltpu.make_async_copy(source.at[part], target.at[part], sems.at[i]))
    for copy in copies:
        copy.start()
    owner = owner_ref[0]
    rows = rows_ref[:, :width]

    choices = ids_ref[:, ids_ref.shape[1] - lanes :].astype(jnp.float32)
    names = lax.broadcasted_iota(jnp.int32, (total_rows, expert_count), 1)
    member = jnp.zeros((total_rows, expert_count), jnp.bool_)
    for k in range(top_count):
        at = micro_index * top_count + k
        member = member | (choices[:, at : at + 1] == names.astype(jnp.float32))
    mine = names == owner
    row_at = lax.broadcasted_iota(jnp.int32, (total_rows, total_rows), 0)
    column_at = lax.broadcasted_iota(jnp.int32, (total_rows, total_rows), 1)
    before = (column_at < row_at) & (column_at // row_count == row_at // row_count)
    named = jnp.where(member & mine, 1.0, 0.0)
    earlier = jnp.dot(
        jnp.where(before, 1.0, 0.0).astype(jnp.bfloat16), named.astype(jnp.bfloat16), preferred_element_type=jnp.float32
    )
    kept = jnp.sum(jnp.where((named > 0.5) & (earlier < capacity - 0.5), 1.0, 0.0), axis=1, keepdims=True)
    logits = lax.dot_general(rows, router_ref[...], (((1,), (1,)), ((), ())), preferred_element_type=jnp.float32)
    scores = jax.nn.sigmoid(logits)
    total = jnp.sum(jnp.where(member, scores, 0.0), axis=1, keepdims=True)
    own = jnp.sum(jnp.where(mine, scores, 0.0), axis=1, keepdims=True)
    factor = jnp.where(kept > 0.5, routed_scale * own / total, 0.0)

    for at in range(0, inner_width, inner_step):
        copies.pop(0).wait()
        copies.pop(0).wait()
        gate_part = jnp.dot(rows, gate_ref[:, at : at + inner_step], preferred_element_type=jnp.float32)
        up_part = jnp.dot(rows, up_ref[:, at : at + inner_step], preferred_element_type=jnp.float32)
        hidden = (gate_part / (1.0 + jnp.exp(-gate_part)) * up_part).astype(jnp.bfloat16)
        hidden_ref[:, at : at + inner_step] = hidden
    hidden = hidden_ref[...]
    for at in range(0, width, outer_step):
        copies.pop(0).wait()
        part = jnp.dot(hidden, down_ref[:, at : at + outer_step], preferred_element_type=jnp.float32) * factor
        part = part.reshape(inner_size, outer, row_count, outer_step)
        part = jnp.concatenate([part[:, o] for o in range(outer)], axis=0).reshape(total_rows, outer_step)
        out_ref[:, at : at + outer_step] = part.astype(jnp.bfloat16)


def expert_shares(micro_index, top_count, row_count, capacity, owner, rows, ids, router_rows, weights):
    total_rows = rows.shape[0]
    inner_width, width = weights[2].shape
    in_vmem = pl.BlockSpec(memory_space=pltpu.VMEM)
    return pl.pallas_call(
        functools.partial(
            expert_kernel, micro_index, top_count, row_count, capacity, total_rows // row_count // inner_size
        ),
        out_shape=jax.ShapeDtypeStruct((total_rows, width), jnp.bfloat16),
        in_specs=[pl.BlockSpec(memory_space=pltpu.SMEM)] + [in_vmem] * 3 + [pl.BlockSpec(memory_space=pltpu.HBM)] * 3,
        out_specs=in_vmem,
        scratch_shapes=[pltpu.VMEM(w.shape, w.dtype) for w in weights]
        + [
            pltpu.VMEM((total_rows, inner_width), jnp.bfloat16),
            pltpu.SemaphoreType.DMA((2 * (inner_width // 256) + width // 512,)),
        ],
        compiler_params=pltpu.CompilerParams(vmem_limit_bytes=36 * 1024 * 1024),
        cost_estimate=pl.CostEstimate(
            flops=6 * total_rows * width * inner_width,
            bytes_accessed=6 * width * inner_width + 4 * total_rows * width,
            transcendentals=0,
        ),
    )(owner, rows, ids, router_rows, *weights)


def per_device(tokens, norm_gain, router, w_gate, w_up, w_down, expert_ids):
    sections = lax.axis_size("section")
    section_index = lax.axis_index("section")
    expert_count = lax.axis_size("expert")
    owner = lax.axis_index("expert").astype(jnp.int32).reshape(1)
    micro_count = expert_ids.shape[1]
    row_count = tokens.shape[1]
    width = tokens.shape[2]
    top_count = expert_ids.shape[3]
    capacity = min(row_count, max(2, 5 * row_count * top_count // (4 * expert_count)))

    router_rows = jnp.transpose(router[0])
    weights = [pltpu.with_memory_space_constraint(w[0, 0], pltpu.HBM) for w in (w_gate, w_up, w_down)]

    hidden = [
        tokens[0] if m == 0 else lax.ppermute(tokens[0], "section", [(m, 0)]) for m in range(micro_count)
    ]
    ids = None

    def send_back(shares):
        shares = shares.reshape(expert_count, row_count, width)
        return lax.all_to_all(shares, "expert", split_axis=0, concat_axis=0, tiled=True)

    def finish(layer, m, returned):
        branch = jnp.sum(returned.astype(jnp.float32), axis=0)
        result = (hidden[m].astype(jnp.float32) + branch).astype(jnp.bfloat16)
        goal = layer + 1 if layer < sections - 1 else m
        return result if goal == layer else lax.ppermute(result, "section", [(layer, goal)])

    for layer in range(sections):
        for m in range(micro_count):
            if m > 0:
                hidden[m], shares = lax.optimization_barrier((hidden[m], shares))
                returned = send_back(shares)
            if ids is None:
                rows = ids = gather_rows(normalize(hidden[m], norm_gain, expert_ids[0]))
            else:
                rows = gather_rows(normalize(hidden[m], norm_gain))
            if m > 0:
                hidden[m - 1] = finish(layer, m - 1, returned)
            elif layer > 0:
                rows, returned = lax.optimization_barrier((rows, returned))
                hidden[-1] = finish(layer - 1, micro_count - 1, returned)
            shares = expert_shares(m, top_count, row_count, capacity, owner, rows, ids, router_rows, weights)
        returned = send_back(shares)
    hidden[-1] = finish(sections - 1, micro_count - 1, returned)
    mixed = hidden[0]
    for m in range(1, micro_count):
        mixed = jnp.where(section_index == m, hidden[m], mixed)
    return mixed[None]


def solution(mesh):
    placed = (
        P("section", "expert", None),
        P("section", None),
        P("section", None, None),
        P("section", "expert", None, None),
        P("section", "expert", None, None),
        P("section", "expert", None, None),
        P("section", None, "expert", None),
    )
    return jax.shard_map(
        per_device,
        mesh=mesh,
        in_specs=placed,
        out_specs=P("section", "expert", None),
        check_vma=False,
    )
```

```python
import functools

import jax
import jax.numpy as jnp
from jax import lax
from jax.experimental import pallas as pl
from jax.experimental.pallas import tpu as pltpu
from jax.sharding import PartitionSpec as P

epsilon = 1e-06
routed_scale = 2.5
lanes = 128
group = 8
in_smem = pl.BlockSpec(memory_space=pltpu.SMEM)
in_vmem = pl.BlockSpec(memory_space=pltpu.VMEM)
in_hbm = pl.BlockSpec(memory_space=pltpu.HBM)


def hbm(array):
    return pltpu.with_memory_space_constraint(array, pltpu.HBM)


def tile_count(capacity, width):
    return -(-capacity * (width // lanes) // group)


def chunks_in_tile(tile, capacity, width):
    last = min(group * tile + group - 1, capacity * (width // lanes) - 1)
    return range(group * tile // capacity, last // capacity + 1)


def normalize(values, gain):
    inverse_rms = lax.rsqrt(jnp.mean(values * values, axis=-1, keepdims=True) + epsilon)
    return (values * inverse_rms * gain).astype(jnp.bfloat16)


def first_norm_kernel(tokens_hbm, gain_hbm, ids_hbm, out_ref, tokens_ref, gain_ref, ids_ref, sems):
    copies = [
        pltpu.make_async_copy(source, target, sems.at[i])
        for i, (source, target) in enumerate(((tokens_hbm, tokens_ref), (gain_hbm, gain_ref), (ids_hbm, ids_ref)))
    ]
    for copy in copies:
        copy.start()
    for copy in copies:
        copy.wait()
    row_count, width = tokens_ref.shape
    out_ref[:, :width] = normalize(tokens_ref[...].astype(jnp.float32), gain_ref[...].astype(jnp.float32))
    micro_count, _, top_count = ids_ref.shape
    lane_at = lax.broadcasted_iota(jnp.int32, (row_count, lanes), 1)
    named = jnp.zeros((row_count, lanes), jnp.float32)
    for m in range(micro_count):
        choices = ids_ref[m].astype(jnp.float32)
        for k in range(top_count):
            named = jnp.where(lane_at == m * top_count + k, choices[:, k : k + 1], named)
    out_ref[:, width:] = named.astype(jnp.bfloat16)


def first_norm(tokens, gain, ids):
    return pl.pallas_call(
        first_norm_kernel,
        out_shape=jax.ShapeDtypeStruct((tokens.shape[0], tokens.shape[1] + lanes), jnp.bfloat16),
        in_specs=[in_hbm] * 3,
        out_specs=in_vmem,
        scratch_shapes=[pltpu.VMEM(x.shape, x.dtype) for x in (tokens, gain, ids)] + [pltpu.SemaphoreType.DMA((3,))],
        compiler_params=pltpu.CompilerParams(vmem_limit_bytes=4 * 1024 * 1024),
    )(hbm(tokens), hbm(gain), hbm(ids))


def norm_kernel(hidden_ref, gain_ref, out_ref):
    out_ref[...] = normalize(hidden_ref[...].astype(jnp.float32), gain_ref[...].astype(jnp.float32))


def later_norm(hidden, gain):
    return pl.pallas_call(
        norm_kernel,
        out_shape=jax.ShapeDtypeStruct(hidden.shape, jnp.bfloat16),
        in_specs=[in_vmem] * 2,
        out_specs=in_vmem,
        compiler_params=pltpu.CompilerParams(vmem_limit_bytes=4 * 1024 * 1024),
    )(hidden, gain)


def expert_kernel(
    micro_count, top_count, row_count, capacity,
    place_ref, rows_ref, ids_ref, router_hbm, gate_hbm, up_hbm, down_hbm, out_ref,
    router_ref, gate_ref, up_ref, down_ref, gate_sum, up_sum, y_ref, sems,
):
    total_rows, width = y_ref.shape
    expert_count = router_ref.shape[0]
    inner_width = gate_hbm.shape[1]
    inner_step, outer_step = 512, 512
    everything = slice(None)
    pieces = [(router_hbm, router_ref, (everything,))]
    for at in range(0, width, inner_step):
        pieces += [(source, target, (pl.ds(at, inner_step),)) for source, target in ((gate_hbm, gate_ref), (up_hbm, up_ref))]
    pieces += [(down_hbm, down_ref, (everything, pl.ds(at, outer_step))) for at in range(0, width, outer_step)]
    copies = [
        pltpu.make_async_copy(source.at[part], target.at[part], sems.at[i])
        for i, (source, target, part) in enumerate(pieces)
    ]
    for copy in copies:
        copy.start()

    owner, micro = place_ref[0], place_ref[1]
    ids = ids_ref[:, ids_ref.shape[1] - lanes :].astype(jnp.float32)
    names = lax.broadcasted_iota(jnp.int32, (total_rows, expert_count), 1).astype(jnp.float32)
    member = jnp.zeros((total_rows, expert_count), jnp.float32)
    for k in range(top_count):
        choice = ids[:, k : k + 1]
        for m in range(1, micro_count):
            at = m * top_count + k
            choice = jnp.where(micro == m, ids[:, at : at + 1], choice)
        member = jnp.where(choice == names, 1.0, member)
    mine = names == owner.astype(jnp.float32)
    row_at = lax.broadcasted_iota(jnp.int32, (total_rows, total_rows), 0)
    column_at = lax.broadcasted_iota(jnp.int32, (total_rows, total_rows), 1)
    same_block = column_at // row_count == row_at // row_count
    before = jnp.where((column_at < row_at) & same_block, 1.0, 0.0).astype(jnp.bfloat16)
    named = jnp.where(mine, member, 0.0)
    earlier = jnp.dot(before, named.astype(jnp.bfloat16), preferred_element_type=jnp.float32)
    slot = jnp.sum(jnp.where(mine, earlier, 0.0), axis=1, keepdims=True)
    named = jnp.sum(named, axis=1, keepdims=True)
    kept = (named > 0.5) & (slot < capacity - 0.5)
    picks = same_block & (slot == (column_at % row_count).astype(jnp.float32)) & kept
    picks = jnp.transpose(jnp.where(picks, 1.0, 0.0)).astype(jnp.bfloat16)

    copies.pop(0).wait()
    logits = lax.dot_general(
        rows_ref[:, :width], router_ref[...], (((1,), (1,)), ((), ())), preferred_element_type=jnp.float32
    )
    scores = jax.nn.sigmoid(logits)
    total = jnp.sum(jnp.where(member > 0.5, scores, 0.0), axis=1, keepdims=True)
    own = jnp.sum(jnp.where(mine, scores, 0.0), axis=1, keepdims=True)
    factor = routed_scale * own / total

    for at in range(0, width, inner_step):
        part = slice(at, at + inner_step)
        for weight_ref, sum_ref in ((gate_ref, gate_sum), (up_ref, up_sum)):
            copies.pop(0).wait()
            product = jnp.dot(rows_ref[:, part], weight_ref[part, :], preferred_element_type=jnp.float32)
            sum_ref[...] = product if at == 0 else sum_ref[...] + product
    gate_part = gate_sum[...]
    hidden = gate_part / (1.0 + jnp.exp(-gate_part)) * up_sum[...] * factor
    slots = jnp.dot(picks, hidden.astype(jnp.bfloat16), preferred_element_type=jnp.float32).astype(jnp.bfloat16)

    blocks = total_rows // group
    row_in_tile = lax.broadcasted_iota(jnp.int32, (blocks, group, lanes), 1)
    tile = 0
    for at in range(0, width, outer_step):
        copies.pop(0).wait()
        part = slice(at, at + outer_step)
        y_ref[:, part] = jnp.dot(slots, down_ref[:, part], preferred_element_type=jnp.float32)
        while tile < tile_count(capacity, width) and chunks_in_tile(tile, capacity, width)[-1] < (at + outer_step) // lanes:
            packed = jnp.zeros((blocks, group, lanes), jnp.float32)
            for chunk in chunks_in_tile(tile, capacity, width):
                shift = chunk * capacity - group * tile
                piece = y_ref[:, chunk * lanes : (chunk + 1) * lanes].reshape(blocks, group, lanes)
                if shift % group:
                    piece = pltpu.roll(piece, shift % group, 1)
                packed = jnp.where((row_in_tile >= shift) & (row_in_tile < shift + capacity), piece, packed)
            out_ref[:, tile * lanes : (tile + 1) * lanes] = packed.reshape(total_rows, lanes).astype(jnp.bfloat16)
            tile += 1


def expert_shares(micro_count, top_count, row_count, capacity, place, rows, ids, router_rows, weights):
    total_rows = rows.shape[0]
    inner_width, width = weights[2].shape
    out_width = lanes * tile_count(capacity, width)
    return pl.pallas_call(
        functools.partial(expert_kernel, micro_count, top_count, row_count, capacity),
        out_shape=jax.ShapeDtypeStruct((total_rows, out_width), jnp.bfloat16),
        in_specs=[in_smem, in_vmem, in_vmem] + [in_hbm] * 4,
        out_specs=in_vmem,
        scratch_shapes=[pltpu.VMEM(w.shape, w.dtype) for w in (router_rows, *weights)]
        + [pltpu.VMEM((total_rows, inner_width), jnp.float32)] * 2
        + [pltpu.VMEM((total_rows, width), jnp.float32), pltpu.SemaphoreType.DMA((1 + 3 * (width // 512),))],
        compiler_params=pltpu.CompilerParams(vmem_limit_bytes=36 * 1024 * 1024),
        cost_estimate=pl.CostEstimate(
            flops=6 * total_rows * width * inner_width, bytes_accessed=6 * width * inner_width, transcendentals=0
        ),
    )(place, rows, ids, hbm(router_rows), *[hbm(w) for w in weights])


def sum_kernel(capacity, place_ref, returned_ref, ids_ref, hidden_ref, out_ref):
    micro_count, row_count, top_count = ids_ref.shape
    width = hidden_ref.shape[1]
    total = returned_ref.shape[0]
    micro = place_ref[1]
    lane_at = lax.broadcasted_iota(jnp.int32, (row_count, total), 1)
    row_at = lax.broadcasted_iota(jnp.int32, (row_count, total), 0)
    ids = ids_ref[0]
    for m in range(1, micro_count):
        ids = jnp.where(micro == m, ids_ref[m], ids)
    member = jnp.zeros((row_count, total), jnp.float32)
    for k in range(top_count):
        member = jnp.where(ids[:, k : k + 1] == lane_at // group, 1.0, member)
    slot = jnp.zeros((row_count, total), jnp.float32)
    for i in range(row_count - 1):
        slot = slot + jnp.where(row_at > i, member[i : i + 1, :], 0.0)
    slot = jnp.where(member > 0.5, slot, -1.0).astype(jnp.int32)
    sums = {}
    for tile in range(tile_count(capacity, width)):
        picks = []
        for chunk in chunks_in_tile(tile, capacity, width):
            wanted = lane_at % group + (group * tile - chunk * capacity)
            picks.append(jnp.where((slot == wanted) & (wanted >= 0) & (wanted < capacity), 1.0, 0.0))
        shares = returned_ref[:, tile * lanes : (tile + 1) * lanes]
        found = jnp.dot(jnp.concatenate(picks, axis=0).astype(jnp.bfloat16), shares, preferred_element_type=jnp.float32)
        for i, chunk in enumerate(chunks_in_tile(tile, capacity, width)):
            piece = found[i * row_count : (i + 1) * row_count]
            sums[chunk] = sums[chunk] + piece if chunk in sums else piece
    for chunk, branch in sums.items():
        part = slice(chunk * lanes, (chunk + 1) * lanes)
        out_ref[:, part] = (hidden_ref[:, part].astype(jnp.float32) + branch).astype(jnp.bfloat16)


def add_shares(capacity, place, returned, ids, hidden):
    return pl.pallas_call(
        functools.partial(sum_kernel, capacity),
        out_shape=jax.ShapeDtypeStruct(hidden.shape, jnp.bfloat16),
        in_specs=[in_smem] + [in_vmem] * 3,
        out_specs=in_vmem,
        compiler_params=pltpu.CompilerParams(vmem_limit_bytes=6 * 1024 * 1024),
    )(place, returned, ids, hidden)


def per_device(tokens, norm_gain, router, w_gate, w_up, w_down, expert_ids):
    sections = lax.axis_size("section")
    section_index = lax.axis_index("section")
    expert_count = lax.axis_size("expert")
    owner = lax.axis_index("expert")
    micro_count = expert_ids.shape[1]
    row_count = tokens.shape[1]
    width = tokens.shape[2]
    top_count = expert_ids.shape[3]
    capacity = min(row_count, max(2, 5 * row_count * top_count // (4 * expert_count)))
    router_rows = jnp.transpose(router[0])
    weights = [w[0, 0] for w in (w_gate, w_up, w_down)]
    own_ids = expert_ids[0]

    incoming = tokens[0]
    mixed = tokens[0]
    ids = None
    total_moments = sections + micro_count - 1
    for moment in range(total_moments):
        micro = jnp.clip(moment - section_index, 0, micro_count - 1)
        place = jnp.stack([owner, micro]).astype(jnp.int32)
        if moment == 0:
            normed = first_norm(incoming, norm_gain, own_ids)
        else:
            normed = later_norm(incoming, norm_gain)
        rows = lax.all_gather(normed, "expert", axis=0, tiled=True)
        ids = rows if ids is None else ids
        shares = expert_shares(micro_count, top_count, row_count, capacity, place, rows, ids, router_rows, weights)
        waiting = None
        if moment + 1 < micro_count:
            shares, waiting = lax.optimization_barrier((shares, tokens[0]))
            waiting = lax.ppermute(waiting, "section", [(moment + 1, 0)])
        returned = lax.all_to_all(
            shares.reshape(expert_count, group, shares.shape[1]), "expert", split_axis=0, concat_axis=0, tiled=True
        )
        result = add_shares(capacity, place, returned.reshape(shares.shape), own_ids, incoming)

        finished = moment - (sections - 1)
        route = [(s, s + 1) for s in range(sections - 1)]
        if finished == sections - 1:
            mixed = jnp.where(section_index == finished, result, mixed)
        elif finished == 0:
            route.append((sections - 1, 0))
        elif finished > 0:
            mixed = jnp.where(section_index == finished, lax.ppermute(result, "section", [(sections - 1, finished)]), mixed)
        if moment < total_moments - 1:
            incoming = lax.ppermute(result, "section", route)
            if finished == 0:
                mixed = jnp.where(section_index == 0, incoming, mixed)
            if waiting is not None:
                incoming = jnp.where(section_index == 0, waiting, incoming)
    return mixed[None]


def solution(mesh):
    placed = (
        P("section", "expert", None),
        P("section", None),
        P("section", None, None),
        P("section", "expert", None, None),
        P("section", "expert", None, None),
        P("section", "expert", None, None),
        P("section", None, "expert", None),
    )
    return jax.shard_map(
        per_device,
        mesh=mesh,
        in_specs=placed,
        out_specs=P("section", "expert", None),
        check_vma=False,
    )
```

```python
import functools

import jax
import jax.numpy as jnp
from jax import lax
from jax.experimental import pallas as pl
from jax.experimental.pallas import tpu as pltpu
from jax.sharding import PartitionSpec as P

epsilon = 1e-06
routed_scale = 2.5
lanes = 128
group = 8
in_smem = pl.BlockSpec(memory_space=pltpu.SMEM)
in_vmem = pl.BlockSpec(memory_space=pltpu.VMEM)
in_hbm = pl.BlockSpec(memory_space=pltpu.HBM)


def hbm(array):
    return pltpu.with_memory_space_constraint(array, pltpu.HBM)


def tile_count(capacity, width):
    return -(-capacity * (width // lanes) // group)


def chunks_in_tile(tile, capacity, width):
    last = min(group * tile + group - 1, capacity * (width // lanes) - 1)
    return range(group * tile // capacity, last // capacity + 1)


def micro_at(moment, micro_count, place_ref):
    return jnp.minimum(jnp.maximum(moment - place_ref[1], 0), micro_count - 1)


def normalize(values, gain):
    inverse_rms = lax.rsqrt(jnp.mean(values * values, axis=-1, keepdims=True) + epsilon)
    return (values * inverse_rms * gain).astype(jnp.bfloat16)


def first_norm_kernel(tokens_hbm, gain_hbm, ids_hbm, out_ref, tokens_ref, gain_ref, ids_ref, sems):
    copies = [
        pltpu.make_async_copy(source, target, sems.at[i])
        for i, (source, target) in enumerate(((tokens_hbm, tokens_ref), (gain_hbm, gain_ref), (ids_hbm, ids_ref)))
    ]
    for copy in copies:
        copy.start()
    for copy in copies:
        copy.wait()
    row_count, width = tokens_ref.shape
    out_ref[:, :width] = normalize(tokens_ref[...].astype(jnp.float32), gain_ref[...].astype(jnp.float32))
    micro_count, _, top_count = ids_ref.shape
    lane_at = lax.broadcasted_iota(jnp.int32, (row_count, lanes), 1)
    named = jnp.zeros((row_count, lanes), jnp.float32)
    for m in range(micro_count):
        choices = ids_ref[m].astype(jnp.float32)
        for k in range(top_count):
            named = jnp.where(lane_at == m * top_count + k, choices[:, k : k + 1], named)
    out_ref[:, width:] = named.astype(jnp.bfloat16)


def first_norm(tokens, gain, ids):
    return pl.pallas_call(
        first_norm_kernel,
        out_shape=jax.ShapeDtypeStruct((tokens.shape[0], tokens.shape[1] + lanes), jnp.bfloat16),
        in_specs=[in_hbm] * 3,
        out_specs=in_vmem,
        scratch_shapes=[pltpu.VMEM(x.shape, x.dtype) for x in (tokens, gain, ids)] + [pltpu.SemaphoreType.DMA((3,))],
        compiler_params=pltpu.CompilerParams(vmem_limit_bytes=4 * 1024 * 1024),
    )(hbm(tokens), hbm(gain), hbm(ids))


def norm_kernel(place_ref, hidden_ref, gain_ref, *rest):
    *waiting, out_ref, hidden_out = rest
    hidden = hidden_ref[...]
    if waiting:
        hidden = jnp.where(place_ref[1] == 0, waiting[0][...], hidden)
    hidden_out[...] = hidden
    out_ref[...] = normalize(hidden.astype(jnp.float32), gain_ref[...].astype(jnp.float32))


def later_norm(place, hidden, gain, *waiting):
    return pl.pallas_call(
        norm_kernel,
        out_shape=[jax.ShapeDtypeStruct(hidden.shape, jnp.bfloat16)] * 2,
        in_specs=[in_smem] + [in_vmem] * (2 + len(waiting)),
        out_specs=[in_vmem] * 2,
        compiler_params=pltpu.CompilerParams(vmem_limit_bytes=4 * 1024 * 1024),
    )(place, hidden, gain, *waiting)


def expert_kernel(
    moment, micro_count, top_count, row_count, capacity,
    place_ref, rows_ref, ids_ref, router_hbm, gate_hbm, up_hbm, down_hbm, out_ref,
    gate_sum, up_sum, y_ref,
):
    total_rows, width = y_ref.shape
    inner_width = gate_hbm.shape[1]
    inner_step, outer_step = 512, 512
    router_ref, gate_ref, up_ref, down_ref = router_hbm, gate_hbm, up_hbm, down_hbm
    expert_count = router_ref.shape[0]

    owner, micro = place_ref[0], micro_at(moment, micro_count, place_ref)
    ids = ids_ref[:, ids_ref.shape[1] - lanes :].astype(jnp.float32)
    names = lax.broadcasted_iota(jnp.int32, (total_rows, expert_count), 1).astype(jnp.float32)
    member = jnp.zeros((total_rows, expert_count), jnp.float32)
    for k in range(top_count):
        choice = ids[:, k : k + 1]
        for m in range(1, micro_count):
            at = m * top_count + k
            choice = jnp.where(micro == m, ids[:, at : at + 1], choice)
        member = jnp.where(choice == names, 1.0, member)
    mine = names == owner.astype(jnp.float32)
    row_at = lax.broadcasted_iota(jnp.int32, (total_rows, total_rows), 0)
    column_at = lax.broadcasted_iota(jnp.int32, (total_rows, total_rows), 1)
    same_block = column_at // row_count == row_at // row_count
    before = jnp.where((column_at < row_at) & same_block, 1.0, 0.0).astype(jnp.bfloat16)
    named = jnp.where(mine, member, 0.0)
    earlier = jnp.dot(before, named.astype(jnp.bfloat16), preferred_element_type=jnp.float32)
    slot = jnp.sum(jnp.where(mine, earlier, 0.0), axis=1, keepdims=True)
    named = jnp.sum(named, axis=1, keepdims=True)
    kept = (named > 0.5) & (slot < capacity - 0.5)
    picks = same_block & (slot == (column_at % row_count).astype(jnp.float32)) & kept
    picks = jnp.transpose(jnp.where(picks, 1.0, 0.0)).astype(jnp.bfloat16)

    logits = lax.dot_general(
        rows_ref[:, :width], router_ref[...], (((1,), (1,)), ((), ())), preferred_element_type=jnp.float32
    )
    scores = jax.nn.sigmoid(logits)
    total = jnp.sum(jnp.where(member > 0.5, scores, 0.0), axis=1, keepdims=True)
    own = jnp.sum(jnp.where(mine, scores, 0.0), axis=1, keepdims=True)
    factor = routed_scale * own / total

    for at in range(0, width, inner_step):
        part = slice(at, at + inner_step)
        for weight_ref, sum_ref in ((gate_ref, gate_sum), (up_ref, up_sum)):
            product = jnp.dot(rows_ref[:, part], weight_ref[part, :], preferred_element_type=jnp.float32)
            sum_ref[...] = product if at == 0 else sum_ref[...] + product
    gate_part = gate_sum[...]
    hidden = gate_part / (1.0 + jnp.exp(-gate_part)) * up_sum[...] * factor
    slots = jnp.dot(picks, hidden.astype(jnp.bfloat16), preferred_element_type=jnp.float32).astype(jnp.bfloat16)

    blocks = total_rows // group
    row_in_tile = lax.broadcasted_iota(jnp.int32, (blocks, group, lanes), 1)
    tile = 0
    for at in range(0, width, outer_step):
        part = slice(at, at + outer_step)
        y_ref[:, part] = jnp.dot(slots, down_ref[:, part], preferred_element_type=jnp.float32)
        while tile < tile_count(capacity, width) and chunks_in_tile(tile, capacity, width)[-1] < (at + outer_step) // lanes:
            packed = jnp.zeros((blocks, group, lanes), jnp.float32)
            for chunk in chunks_in_tile(tile, capacity, width):
                shift = chunk * capacity - group * tile
                piece = y_ref[:, chunk * lanes : (chunk + 1) * lanes].reshape(blocks, group, lanes)
                if shift % group:
                    piece = pltpu.roll(piece, shift % group, 1)
                packed = jnp.where((row_in_tile >= shift) & (row_in_tile < shift + capacity), piece, packed)
            out_ref[:, tile * lanes : (tile + 1) * lanes] = packed.reshape(total_rows, lanes).astype(jnp.bfloat16)
            tile += 1


def expert_shares(moment, micro_count, top_count, row_count, capacity, place, rows, ids, router_rows, weights):
    total_rows = rows.shape[0]
    inner_width, width = weights[2].shape
    out_width = lanes * tile_count(capacity, width)
    return pl.pallas_call(
        functools.partial(expert_kernel, moment, micro_count, top_count, row_count, capacity),
        out_shape=jax.ShapeDtypeStruct((total_rows, out_width), jnp.bfloat16),
        in_specs=[in_smem, in_vmem, in_vmem] + [in_vmem] * 4,
        out_specs=in_vmem,
        scratch_shapes=[pltpu.VMEM((total_rows, inner_width), jnp.float32)] * 2
        + [pltpu.VMEM((total_rows, width), jnp.float32)],
        compiler_params=pltpu.CompilerParams(vmem_limit_bytes=10 * 1024 * 1024),
        cost_estimate=pl.CostEstimate(
            flops=6 * total_rows * width * inner_width, bytes_accessed=6 * width * inner_width, transcendentals=0
        ),
    )(place, rows, ids, router_rows, *weights)


def sum_kernel(moment, capacity, own_section, place_ref, returned_ref, ids_ref, hidden_ref, *rest):
    *kept, out_ref = rest
    micro_count, row_count, top_count = ids_ref.shape
    width = hidden_ref.shape[1]
    total = returned_ref.shape[0]
    micro = micro_at(moment, micro_count, place_ref)
    lane_at = lax.broadcasted_iota(jnp.int32, (row_count, total), 1)
    row_at = lax.broadcasted_iota(jnp.int32, (row_count, total), 0)
    ids = ids_ref[0]
    for m in range(1, micro_count):
        ids = jnp.where(micro == m, ids_ref[m], ids)
    member = jnp.zeros((row_count, total), jnp.float32)
    for k in range(top_count):
        member = jnp.where(ids[:, k : k + 1] == lane_at // group, 1.0, member)
    slot = jnp.zeros((row_count, total), jnp.float32)
    for i in range(row_count - 1):
        slot = slot + jnp.where(row_at > i, member[i : i + 1, :], 0.0)
    slot = jnp.where(member > 0.5, slot, -1.0).astype(jnp.int32)
    sums = {}
    for tile in range(tile_count(capacity, width)):
        picks = []
        for chunk in chunks_in_tile(tile, capacity, width):
            wanted = lane_at % group + (group * tile - chunk * capacity)
            picks.append(jnp.where((slot == wanted) & (wanted >= 0) & (wanted < capacity), 1.0, 0.0))
        shares = returned_ref[:, tile * lanes : (tile + 1) * lanes]
        found = jnp.dot(jnp.concatenate(picks, axis=0).astype(jnp.bfloat16), shares, preferred_element_type=jnp.float32)
        for i, chunk in enumerate(chunks_in_tile(tile, capacity, width)):
            piece = found[i * row_count : (i + 1) * row_count]
            sums[chunk] = sums[chunk] + piece if chunk in sums else piece
    for chunk, branch in sums.items():
        part = slice(chunk * lanes, (chunk + 1) * lanes)
        result = (hidden_ref[:, part].astype(jnp.float32) + branch).astype(jnp.bfloat16)
        if kept:
            result = jnp.where(place_ref[1] == own_section, result, kept[0][:, part])
        out_ref[:, part] = result


def add_shares(moment, capacity, own_section, place, returned, ids, hidden, *kept):
    return pl.pallas_call(
        functools.partial(sum_kernel, moment, capacity, own_section),
        out_shape=jax.ShapeDtypeStruct(hidden.shape, jnp.bfloat16),
        in_specs=[in_smem] + [in_vmem] * (3 + len(kept)),
        out_specs=in_vmem,
        compiler_params=pltpu.CompilerParams(vmem_limit_bytes=6 * 1024 * 1024),
    )(place, returned, ids, hidden, *kept)


def per_device(tokens, norm_gain, router, w_gate, w_up, w_down, expert_ids):
    sections = lax.axis_size("section")
    section_index = lax.axis_index("section")
    expert_count = lax.axis_size("expert")
    owner = lax.axis_index("expert")
    micro_count = expert_ids.shape[1]
    row_count = tokens.shape[1]
    width = tokens.shape[2]
    top_count = expert_ids.shape[3]
    capacity = min(row_count, max(2, 5 * row_count * top_count // (4 * expert_count)))
    router_rows = jnp.transpose(router[0])
    weights = [w[0, 0] for w in (w_gate, w_up, w_down)]
    own_ids = expert_ids[0]

    place = jnp.stack([owner, section_index]).astype(jnp.int32)
    incoming = tokens[0]
    mixed = ids = None
    final = sections - 1
    total_moments = sections + micro_count - 1
    for moment in range(total_moments):
        if moment == 0:
            normed = first_norm(incoming, norm_gain, own_ids)
        else:
            normed, incoming = later_norm(place, incoming, norm_gain, *waiting)
        rows = lax.all_gather(normed, "expert", axis=0, tiled=True)
        ids = rows if ids is None else ids
        shares = expert_shares(moment, micro_count, top_count, row_count, capacity, place, rows, ids, router_rows, weights)
        returned = lax.all_to_all(
            shares.reshape(expert_count, group, shares.shape[1]), "expert", split_axis=0, concat_axis=0, tiled=True
        ).reshape(shares.shape)
        route = [(s, s + 1) for s in range(sections - 1)]
        own_section, kept, waiting = 0, (), ()
        entering, finished = moment + 1, moment - final
        if finished == micro_count - 1:
            own_section, kept = final, () if mixed is None else (mixed,)
        elif entering == final and sections == 2:
            kept = (tokens[0],)
        elif entering < micro_count:
            waiting = (lax.ppermute(tokens[0], "section", [(entering, 0)]),)
        result = add_shares(moment, capacity, own_section, place, returned, own_ids, incoming, *kept)
        if finished == micro_count - 1:
            mixed = result
            break
        if finished == 0 or (entering == final and sections == 2):
            route.append((final, 0))
        incoming = lax.ppermute(result, "section", route)
        if finished == 0:
            mixed = incoming
        elif finished > 0:
            sent = lax.ppermute(result, "section", [(final, finished)])
            mixed = jnp.where(section_index == finished, sent, mixed)
    return mixed[None]


def solution(mesh):
    placed = (
        P("section", "expert", None),
        P("section", None),
        P("section", None, None),
        P("section", "expert", None, None),
        P("section", "expert", None, None),
        P("section", "expert", None, None),
        P("section", None, "expert", None),
    )
    return jax.shard_map(
        per_device,
        mesh=mesh,
        in_specs=placed,
        out_specs=P("section", "expert", None),
        check_vma=False,
    )
```

```python
import functools

import jax
import jax.numpy as jnp
from jax import lax
from jax.experimental import pallas as pl
from jax.experimental.pallas import tpu as pltpu
from jax.sharding import PartitionSpec as P

epsilon = 1e-06
routed_scale = 2.5
lanes = 128
group = 8
outer_size = 4
in_smem = pl.BlockSpec(memory_space=pltpu.SMEM)
in_vmem = pl.BlockSpec(memory_space=pltpu.VMEM)
in_hbm = pl.BlockSpec(memory_space=pltpu.HBM)


def hbm(array):
    return pltpu.with_memory_space_constraint(array, pltpu.HBM)


def tile_count(capacity, width):
    return -(-capacity * (width // lanes) // group)


def chunks_in_tile(tile, capacity, width):
    last = min(group * tile + group - 1, capacity * (width // lanes) - 1)
    return range(group * tile // capacity, last // capacity + 1)


def micro_at(moment, micro_count, place_ref):
    return jnp.minimum(jnp.maximum(moment - place_ref[1], 0), micro_count - 1)


def normalize(values, gain):
    inverse_rms = lax.rsqrt(jnp.mean(values * values, axis=-1, keepdims=True) + epsilon)
    return values * inverse_rms * gain


def start_all(copies):
    for copy in copies:
        copy.start()


def wait_all(copies):
    for copy in copies:
        copy.wait()


def first_norm_kernel(place_ref, tokens_hbm, gain_hbm, ids_hbm, out_ref, place_out, tokens_ref, gain_ref, ids_ref, sems):
    pairs = ((tokens_hbm, tokens_ref), (gain_hbm, gain_ref), (ids_hbm, ids_ref))
    copies = [pltpu.make_async_copy(source, target, sems.at[i]) for i, (source, target) in enumerate(pairs)]
    start_all(copies)
    for i in range(place_ref.shape[0]):
        place_out[i] = place_ref[i]
    wait_all(copies)
    row_count, width = tokens_ref.shape
    out_ref[:, :width] = normalize(tokens_ref[...].astype(jnp.float32), gain_ref[...].astype(jnp.float32)).astype(jnp.bfloat16)
    micro_count, _, top_count = ids_ref.shape
    lane_at = lax.broadcasted_iota(jnp.int32, (row_count, lanes), 1)
    named = jnp.zeros((row_count, lanes), jnp.float32)
    for m in range(micro_count):
        choices = ids_ref[m].astype(jnp.float32)
        for k in range(top_count):
            named = jnp.where(lane_at == m * top_count + k, choices[:, k : k + 1], named)
    out_ref[:, width:] = named.astype(jnp.bfloat16)


def first_norm(place, tokens, gain, ids):
    return pl.pallas_call(
        first_norm_kernel,
        out_shape=[
            jax.ShapeDtypeStruct((tokens.shape[0], tokens.shape[1] + lanes), jnp.bfloat16),
            jax.ShapeDtypeStruct(place.shape, place.dtype),
        ],
        in_specs=[in_smem] + [in_hbm] * 3,
        out_specs=[in_vmem, in_smem],
        scratch_shapes=[pltpu.VMEM(x.shape, x.dtype) for x in (tokens, gain, ids)] + [pltpu.SemaphoreType.DMA((3,))],
        compiler_params=pltpu.CompilerParams(vmem_limit_bytes=4 * 1024 * 1024),
    )(place, hbm(tokens), hbm(gain), hbm(ids))


def hold_kernel(place_ref, *refs):
    count = (len(refs) - 2) // 2
    sources, place_out, targets, sems = refs[:count], refs[count], refs[count + 1 : -1], refs[-1]
    copies = [pltpu.make_async_copy(source, target, sems.at[i]) for i, (source, target) in enumerate(zip(sources, targets))]
    start_all(copies)
    for i in range(place_ref.shape[0]):
        place_out[i] = place_ref[i]
    wait_all(copies)


def hold(place, arrays):
    place, *held = pl.pallas_call(
        hold_kernel,
        out_shape=[jax.ShapeDtypeStruct(x.shape, x.dtype) for x in (place, *arrays)],
        in_specs=[in_smem] + [in_hbm] * len(arrays),
        out_specs=[in_smem] + [in_vmem] * len(arrays),
        scratch_shapes=[pltpu.SemaphoreType.DMA((len(arrays),))],
        compiler_params=pltpu.CompilerParams(vmem_limit_bytes=1024 * 1024),
        cost_estimate=pl.CostEstimate(
            flops=0, bytes_accessed=2 * sum(x.size * x.dtype.itemsize for x in arrays), transcendentals=0
        ),
    )(place, *[hbm(x) for x in arrays])
    return place, held


def order_kernel(norm, inner, place_ref, *refs):
    if norm:
        *refs, gain_ref, out_ref, own_out = refs
    else:
        *refs, out_ref = refs
    outer = outer_size
    blocks = [ref[...].astype(jnp.float32) for ref in refs[:outer]]
    if len(refs) > outer:
        waiting = [ref[...].astype(jnp.float32) for ref in refs[outer:]]
        blocks = [jnp.where(place_ref[1] == 0, w, b) for w, b in zip(waiting, blocks)]
    if norm:
        own_out[...] = blocks[0].astype(jnp.bfloat16)
        blocks = [normalize(b, gain_ref[...].astype(jnp.float32)) for b in blocks]
    here = lax.div(place_ref[0], inner)
    ordered = []
    for at in range(outer):
        back = lax.rem(here - at + outer, outer)
        block = blocks[0]
        for k in range(1, outer):
            block = jnp.where(back == k, blocks[k], block)
        ordered.append(block)
    out_ref[...] = jnp.concatenate(ordered, axis=0).astype(jnp.bfloat16)


def in_order(inner, place, blocks, *gain):
    row_count, width = blocks[0].shape
    out_shape = [jax.ShapeDtypeStruct((outer_size * row_count, width), jnp.bfloat16)]
    if gain:
        out_shape.append(jax.ShapeDtypeStruct((row_count, width), jnp.bfloat16))
    return pl.pallas_call(
        functools.partial(order_kernel, bool(gain), inner),
        out_shape=out_shape,
        in_specs=[in_smem] + [in_vmem] * (len(blocks) + len(gain)),
        out_specs=[in_vmem] * len(out_shape),
        compiler_params=pltpu.CompilerParams(vmem_limit_bytes=6 * 1024 * 1024),
    )(place, *blocks, *gain)


def expert_kernel(
    moment, micro_count, top_count, row_count, capacity,
    place_ref, rows_ref, ids_ref, router_ref, gate_ref, up_ref, down_ref, out_ref, *rest,
):
    inner_width, width = down_ref.shape
    inner_step, outer_step = 512, 512
    copies = []
    if moment == 0:
        down_hbm, (down_ref, *rest, sems) = down_ref, rest
        for i, at in enumerate(range(0, width, outer_step)):
            part = (slice(None), pl.ds(at, outer_step))
            copies.append(pltpu.make_async_copy(down_hbm.at[part], down_ref.at[part], sems.at[i]))
        start_all(copies)
    gate_sum, up_sum, y_ref = rest
    total_rows = y_ref.shape[0]
    expert_count = router_ref.shape[0]
    inner = expert_count // outer_size

    owner, micro = place_ref[0], micro_at(moment, micro_count, place_ref)
    ids = ids_ref[:, ids_ref.shape[1] - lanes :].astype(jnp.float32)
    names = lax.broadcasted_iota(jnp.int32, (total_rows, expert_count), 1).astype(jnp.float32)
    member = jnp.zeros((total_rows, expert_count), jnp.float32)
    for k in range(top_count):
        choice = ids[:, k : k + 1]
        for m in range(1, micro_count):
            at = m * top_count + k
            choice = jnp.where(micro == m, ids[:, at : at + 1], choice)
        member = jnp.where(choice == names, 1.0, member)
    mine = names == owner.astype(jnp.float32)
    row_at = lax.broadcasted_iota(jnp.int32, (total_rows, total_rows), 0)
    column_at = lax.broadcasted_iota(jnp.int32, (total_rows, total_rows), 1)
    block_at = row_at // row_count
    before = (column_at < row_at) & (column_at // row_count == block_at)
    named = jnp.where(mine, member, 0.0)
    earlier = jnp.dot(
        jnp.where(before, 1.0, 0.0).astype(jnp.bfloat16), named.astype(jnp.bfloat16), preferred_element_type=jnp.float32
    )
    slot = jnp.sum(jnp.where(mine, earlier, 0.0), axis=1, keepdims=True)
    named = jnp.sum(named, axis=1, keepdims=True)
    kept = (named > 0.5) & (slot < capacity - 0.5)
    device_at = block_at % outer_size * inner + block_at // outer_size
    picks = (column_at // group == device_at) & (slot == (column_at % group).astype(jnp.float32)) & kept
    picks = jnp.transpose(jnp.where(picks, 1.0, 0.0)).astype(jnp.bfloat16)

    logits = lax.dot_general(
        rows_ref[:, :width], router_ref[...], (((1,), (1,)), ((), ())), preferred_element_type=jnp.float32
    )
    scores = jax.nn.sigmoid(logits)
    total = jnp.sum(jnp.where(member > 0.5, scores, 0.0), axis=1, keepdims=True)
    own = jnp.sum(jnp.where(mine, scores, 0.0), axis=1, keepdims=True)
    factor = routed_scale * own / total

    for at in range(0, width, inner_step):
        part = slice(at, at + inner_step)
        for weight_ref, sum_ref in ((gate_ref, gate_sum), (up_ref, up_sum)):
            product = jnp.dot(rows_ref[:, part], weight_ref[part, :], preferred_element_type=jnp.float32)
            sum_ref[...] = product if at == 0 else sum_ref[...] + product
    gate_part = gate_sum[...]
    hidden = gate_part / (1.0 + jnp.exp(-gate_part)) * up_sum[...] * factor
    slots = jnp.dot(picks, hidden.astype(jnp.bfloat16), preferred_element_type=jnp.float32).astype(jnp.bfloat16)

    blocks = total_rows // group
    row_in_tile = lax.broadcasted_iota(jnp.int32, (blocks, group, lanes), 1)
    tile = 0
    for at in range(0, width, outer_step):
        if copies:
            copies.pop(0).wait()
        part = slice(at, at + outer_step)
        y_ref[:, part] = jnp.dot(slots, down_ref[:, part], preferred_element_type=jnp.float32)
        while tile < tile_count(capacity, width) and chunks_in_tile(tile, capacity, width)[-1] < (at + outer_step) // lanes:
            packed = jnp.zeros((blocks, group, lanes), jnp.float32)
            for chunk in chunks_in_tile(tile, capacity, width):
                shift = chunk * capacity - group * tile
                piece = y_ref[:, chunk * lanes : (chunk + 1) * lanes].reshape(blocks, group, lanes)
                if shift % group:
                    piece = pltpu.roll(piece, shift % group, 1)
                packed = jnp.where((row_in_tile >= shift) & (row_in_tile < shift + capacity), piece, packed)
            out_ref[:, tile * lanes : (tile + 1) * lanes] = packed.reshape(total_rows, lanes).astype(jnp.bfloat16)
            tile += 1


def expert_shares(moment, micro_count, top_count, row_count, capacity, place, rows, ids, weights):
    total_rows = rows.shape[0]
    *held, down = weights
    inner_width, width = down.shape
    out_shape = [jax.ShapeDtypeStruct((total_rows, lanes * tile_count(capacity, width)), jnp.bfloat16)]
    scratch = [pltpu.VMEM((total_rows, inner_width), jnp.float32)] * 2 + [pltpu.VMEM((total_rows, width), jnp.float32)]
    if moment == 0:
        down = hbm(down)
        out_shape.append(jax.ShapeDtypeStruct(down.shape, down.dtype))
        scratch.append(pltpu.SemaphoreType.DMA((width // 512,)))
    shares, *new_down = pl.pallas_call(
        functools.partial(expert_kernel, moment, micro_count, top_count, row_count, capacity),
        out_shape=out_shape,
        in_specs=[in_smem] + [in_vmem] * 5 + [in_hbm if moment == 0 else in_vmem],
        out_specs=[in_vmem] * len(out_shape),
        scratch_shapes=scratch,
        compiler_params=pltpu.CompilerParams(vmem_limit_bytes=10 * 1024 * 1024),
        cost_estimate=pl.CostEstimate(
            flops=6 * total_rows * width * inner_width, bytes_accessed=6 * width * inner_width, transcendentals=0
        ),
    )(place, rows, ids, *held, down)
    return shares, (*held, *(new_down or (down,)))


def sum_kernel(moment, capacity, own_section, place_ref, returned_ref, ids_ref, hidden_ref, *rest):
    *kept, out_ref = rest
    micro_count, row_count, top_count = ids_ref.shape
    width = hidden_ref.shape[1]
    total = returned_ref.shape[0]
    micro = micro_at(moment, micro_count, place_ref)
    lane_at = lax.broadcasted_iota(jnp.int32, (row_count, total), 1)
    row_at = lax.broadcasted_iota(jnp.int32, (row_count, total), 0)
    ids = ids_ref[0]
    for m in range(1, micro_count):
        ids = jnp.where(micro == m, ids_ref[m], ids)
    member = jnp.zeros((row_count, total), jnp.float32)
    for k in range(top_count):
        member = jnp.where(ids[:, k : k + 1] == lane_at // group, 1.0, member)
    slot = jnp.zeros((row_count, total), jnp.float32)
    for i in range(row_count - 1):
        slot = slot + jnp.where(row_at > i, member[i : i + 1, :], 0.0)
    slot = jnp.where(member > 0.5, slot, -1.0).astype(jnp.int32)
    sums = {}
    for tile in range(tile_count(capacity, width)):
        picks = []
        for chunk in chunks_in_tile(tile, capacity, width):
            wanted = lane_at % group + (group * tile - chunk * capacity)
            picks.append(jnp.where((slot == wanted) & (wanted >= 0) & (wanted < capacity), 1.0, 0.0))
        shares = returned_ref[:, tile * lanes : (tile + 1) * lanes]
        found = jnp.dot(jnp.concatenate(picks, axis=0).astype(jnp.bfloat16), shares, preferred_element_type=jnp.float32)
        for i, chunk in enumerate(chunks_in_tile(tile, capacity, width)):
            piece = found[i * row_count : (i + 1) * row_count]
            sums[chunk] = sums[chunk] + piece if chunk in sums else piece
    for chunk, branch in sums.items():
        part = slice(chunk * lanes, (chunk + 1) * lanes)
        result = (hidden_ref[:, part].astype(jnp.float32) + branch).astype(jnp.bfloat16)
        if kept:
            result = jnp.where(place_ref[1] == own_section, result, kept[0][:, part])
        out_ref[:, part] = result


def add_shares(moment, capacity, own_section, place, returned, ids, hidden, *kept):
    return pl.pallas_call(
        functools.partial(sum_kernel, moment, capacity, own_section),
        out_shape=jax.ShapeDtypeStruct(hidden.shape, jnp.bfloat16),
        in_specs=[in_smem] + [in_vmem] * (3 + len(kept)),
        out_specs=in_vmem,
        compiler_params=pltpu.CompilerParams(vmem_limit_bytes=6 * 1024 * 1024),
    )(place, returned, ids, hidden, *kept)


def per_device(tokens, norm_gain, router, w_gate, w_up, w_down, expert_ids):
    sections = lax.axis_size("section")
    section_index = lax.axis_index("section")
    expert_count = lax.axis_size("expert")
    owner = lax.axis_index("expert")
    micro_count = expert_ids.shape[1]
    row_count = tokens.shape[1]
    width = tokens.shape[2]
    top_count = expert_ids.shape[3]
    capacity = min(row_count, max(2, 5 * row_count * top_count // (4 * expert_count)))
    router_rows = jnp.transpose(router[0])
    gate, up, down = (w[0, 0] for w in (w_gate, w_up, w_down))
    own_ids = expert_ids[0]
    inner = expert_count // outer_size
    same_outer = [[o * inner + i for i in range(inner)] for o in range(outer_size)]

    def sent(rows, route, shift):
        pairs = [
            (a * expert_count + e, b * expert_count + (e + shift * inner) % expert_count)
            for a, b in route
            for e in range(expert_count)
        ]
        return lax.ppermute(rows, ("section", "expert"), pairs)

    place = jnp.stack([owner, section_index]).astype(jnp.int32)
    incoming = tokens[0]
    mixed = ids = None
    final = sections - 1
    total_moments = sections + micro_count - 1
    for moment in range(total_moments):
        if moment == 0:
            packed, place = first_norm(place, incoming, norm_gain, own_ids)
            stay = [(s, s) for s in range(sections)]
            blocks = [packed] + [sent(packed, stay, k) for k in range(1, outer_size)]
            place, held = hold(place, (router_rows, gate, up))
            weights = (*held, down)
            (rows,) = in_order(inner, place, blocks)
        else:
            rows, incoming = in_order(inner, place, blocks, norm_gain)
        rows = lax.all_gather(rows, "expert", axis=0, tiled=True, axis_index_groups=same_outer)
        ids = rows if ids is None else ids
        shares, weights = expert_shares(moment, micro_count, top_count, row_count, capacity, place, rows, ids, weights)
        returned = lax.all_to_all(
            shares.reshape(expert_count, group, shares.shape[1]), "expert", split_axis=0, concat_axis=0, tiled=True
        ).reshape(shares.shape)
        route = [(s, s + 1) for s in range(sections - 1)]
        own_section, kept, waiting = 0, (), []
        entering, finished = moment + 1, moment - final
        if finished == micro_count - 1:
            own_section, kept = final, () if mixed is None else (mixed,)
        elif entering == final and sections == 2:
            kept = (tokens[0],)
            route.append((final, 0))
        elif entering < micro_count:
            waiting = [sent(tokens[0], [(entering, 0)], k) for k in range(outer_size)]
        result = add_shares(moment, capacity, own_section, place, returned, own_ids, incoming, *kept)
        if finished == micro_count - 1:
            mixed = result
            break
        own_route = route + [(final, 0)] if finished == 0 else route
        blocks = [sent(result, own_route if k == 0 else route, k) for k in range(outer_size)] + waiting
        if finished == 0:
            mixed = blocks[0]
        elif finished > 0:
            mixed = jnp.where(section_index == finished, sent(result, [(final, finished)], 0), mixed)
    return mixed[None]


def solution(mesh):
    placed = (
        P("section", "expert", None),
        P("section", None),
        P("section", None, None),
        P("section", "expert", None, None),
        P("section", "expert", None, None),
        P("section", "expert", None, None),
        P("section", None, "expert", None),
    )
    return jax.shard_map(
        per_device,
        mesh=mesh,
        in_specs=placed,
        out_specs=P("section", "expert", None),
        check_vma=False,
    )
```

```python
import functools

import jax
import jax.numpy as jnp
from jax import lax
from jax.experimental import pallas as pl
from jax.experimental.pallas import tpu as pltpu
from jax.sharding import PartitionSpec as P

epsilon = 1e-06
routed_scale = 2.5
lanes = 128
group = 8
outer_size = 4
in_vmem = pl.BlockSpec(memory_space=pltpu.VMEM)
in_hbm = pl.BlockSpec(memory_space=pltpu.HBM)


def hbm(array):
    return pltpu.with_memory_space_constraint(array, pltpu.HBM)


def tile_count(capacity, width):
    return -(-capacity * (width // lanes) // group)


def chunks_in_tile(tile, capacity, width):
    last = min(group * tile + group - 1, capacity * (width // lanes) - 1)
    return range(group * tile // capacity, last // capacity + 1)


def owner_of(place_ref):
    return place_ref[0:1, 0:1]


def section_of(place_ref):
    return place_ref[0:1, 1:2]


def micro_at(moment, micro_count, place_ref):
    return jnp.minimum(jnp.maximum(moment - section_of(place_ref), 0), micro_count - 1)


def normalize(values, gain):
    inverse_rms = lax.rsqrt(jnp.mean(values * values, axis=-1, keepdims=True) + epsilon)
    return values * inverse_rms * gain


def start_all(copies):
    for copy in copies:
        copy.start()


def wait_all(copies):
    for copy in copies:
        copy.wait()


def first_norm_kernel(place_ref, tokens_hbm, gain_hbm, ids_hbm, out_ref, place_out, tokens_ref, gain_ref, ids_ref, sems):
    pairs = ((tokens_hbm, tokens_ref), (gain_hbm, gain_ref), (ids_hbm, ids_ref))
    copies = [pltpu.make_async_copy(source, target, sems.at[i]) for i, (source, target) in enumerate(pairs)]
    start_all(copies)
    place_out[...] = place_ref[...]
    wait_all(copies)
    row_count, width = tokens_ref.shape
    out_ref[:, :width] = normalize(tokens_ref[...].astype(jnp.float32), gain_ref[...].astype(jnp.float32)).astype(jnp.bfloat16)
    micro_count, _, top_count = ids_ref.shape
    lane_at = lax.broadcasted_iota(jnp.int32, (row_count, lanes), 1)
    named = jnp.zeros((row_count, lanes), jnp.float32)
    for m in range(micro_count):
        choices = ids_ref[m].astype(jnp.float32)
        for k in range(top_count):
            named = jnp.where(lane_at == m * top_count + k, choices[:, k : k + 1], named)
    out_ref[:, width:] = named.astype(jnp.bfloat16)


def first_norm(place, tokens, gain, ids):
    return pl.pallas_call(
        first_norm_kernel,
        out_shape=[
            jax.ShapeDtypeStruct((tokens.shape[0], tokens.shape[1] + lanes), jnp.bfloat16),
            jax.ShapeDtypeStruct(place.shape, place.dtype),
        ],
        in_specs=[in_vmem] + [in_hbm] * 3,
        out_specs=[in_vmem] * 2,
        scratch_shapes=[pltpu.VMEM(x.shape, x.dtype) for x in (tokens, gain, ids)] + [pltpu.SemaphoreType.DMA((3,))],
        compiler_params=pltpu.CompilerParams(vmem_limit_bytes=4 * 1024 * 1024),
    )(place, hbm(tokens), hbm(gain), hbm(ids))


def hold_kernel(place_ref, *refs):
    count = (len(refs) - 2) // 2
    sources, place_out, targets, sems = refs[:count], refs[count], refs[count + 1 : -1], refs[-1]
    copies = [pltpu.make_async_copy(source, target, sems.at[i]) for i, (source, target) in enumerate(zip(sources, targets))]
    start_all(copies)
    place_out[...] = place_ref[...]
    wait_all(copies)


def hold(place, arrays):
    place, *held = pl.pallas_call(
        hold_kernel,
        out_shape=[jax.ShapeDtypeStruct(x.shape, x.dtype) for x in (place, *arrays)],
        in_specs=[in_vmem] + [in_hbm] * len(arrays),
        out_specs=[in_vmem] * (1 + len(arrays)),
        scratch_shapes=[pltpu.SemaphoreType.DMA((len(arrays),))],
        compiler_params=pltpu.CompilerParams(vmem_limit_bytes=1024 * 1024),
        cost_estimate=pl.CostEstimate(
            flops=0, bytes_accessed=2 * sum(x.size * x.dtype.itemsize for x in arrays), transcendentals=0
        ),
    )(place, *[hbm(x) for x in arrays])
    return place, held


def order_kernel(norm, inner, place_ref, *refs):
    if norm:
        *refs, gain_ref, out_ref, own_out = refs
    else:
        *refs, out_ref = refs
    outer = outer_size
    blocks = [ref[...].astype(jnp.float32) for ref in refs[:outer]]
    if len(refs) > outer:
        waiting = [ref[...].astype(jnp.float32) for ref in refs[outer:]]
        blocks = [jnp.where(section_of(place_ref) == 0, w, b) for w, b in zip(waiting, blocks)]
    if norm:
        own_out[...] = blocks[0].astype(jnp.bfloat16)
        blocks = [normalize(b, gain_ref[...].astype(jnp.float32)) for b in blocks]
    owner = owner_of(place_ref)
    here = [(owner >= o * inner) & (owner < (o + 1) * inner) for o in range(outer)]
    ordered = []
    for at in range(outer):
        block = blocks[0]
        for k in range(1, outer):
            block = jnp.where(here[(at + k) % outer], blocks[k], block)
        ordered.append(block)
    out_ref[...] = jnp.concatenate(ordered, axis=0).astype(jnp.bfloat16)


def in_order(inner, place, blocks, *gain):
    row_count, width = blocks[0].shape
    out_shape = [jax.ShapeDtypeStruct((outer_size * row_count, width), jnp.bfloat16)]
    if gain:
        out_shape.append(jax.ShapeDtypeStruct((row_count, width), jnp.bfloat16))
    return pl.pallas_call(
        functools.partial(order_kernel, bool(gain), inner),
        out_shape=out_shape,
        in_specs=[in_vmem] * (1 + len(blocks) + len(gain)),
        out_specs=[in_vmem] * len(out_shape),
        compiler_params=pltpu.CompilerParams(vmem_limit_bytes=6 * 1024 * 1024),
    )(place, *blocks, *gain)


def expert_kernel(
    moment, micro_count, top_count, row_count, capacity,
    place_ref, rows_ref, ids_ref, router_ref, gate_ref, up_ref, down_ref, out_ref, *rest,
):
    inner_width, width = down_ref.shape
    inner_step, outer_step = 512, 512
    copies = []
    if moment == 0:
        down_hbm, (down_ref, *rest, sems) = down_ref, rest
        for i, at in enumerate(range(0, width, outer_step)):
            part = (slice(None), pl.ds(at, outer_step))
            copies.append(pltpu.make_async_copy(down_hbm.at[part], down_ref.at[part], sems.at[i]))
        start_all(copies)
    hidden_ref, y_ref = rest
    total_rows = y_ref.shape[0]
    expert_count = router_ref.shape[0]
    inner = expert_count // outer_size

    owner, micro = owner_of(place_ref), micro_at(moment, micro_count, place_ref)
    ids = ids_ref[:, ids_ref.shape[1] - lanes :].astype(jnp.float32)
    names = lax.broadcasted_iota(jnp.int32, (total_rows, expert_count), 1).astype(jnp.float32)
    member = jnp.zeros((total_rows, expert_count), jnp.float32)
    for k in range(top_count):
        choice = ids[:, k : k + 1]
        for m in range(1, micro_count):
            at = m * top_count + k
            choice = jnp.where(micro == m, ids[:, at : at + 1], choice)
        member = jnp.where(choice == names, 1.0, member)
    mine = names == owner.astype(jnp.float32)
    row_at = lax.broadcasted_iota(jnp.int32, (total_rows, total_rows), 0)
    column_at = lax.broadcasted_iota(jnp.int32, (total_rows, total_rows), 1)
    block_at = row_at // row_count
    before = (column_at < row_at) & (column_at // row_count == block_at)
    named = jnp.where(mine, member, 0.0)
    earlier = jnp.dot(
        jnp.where(before, 1.0, 0.0).astype(jnp.bfloat16), named.astype(jnp.bfloat16), preferred_element_type=jnp.float32
    )
    slot = jnp.sum(jnp.where(mine, earlier, 0.0), axis=1, keepdims=True)
    named = jnp.sum(named, axis=1, keepdims=True)
    kept = (named > 0.5) & (slot < capacity - 0.5)
    device_at = block_at % outer_size * inner + block_at // outer_size
    picks = (column_at // group == device_at) & (slot == (column_at % group).astype(jnp.float32)) & kept
    picks = jnp.transpose(jnp.where(picks, 1.0, 0.0)).astype(jnp.bfloat16)

    logits = lax.dot_general(
        rows_ref[:, :width], router_ref[...], (((1,), (1,)), ((), ())), preferred_element_type=jnp.float32
    )
    scores = jax.nn.sigmoid(logits)
    total = jnp.sum(jnp.where(member > 0.5, scores, 0.0), axis=1, keepdims=True)
    own = jnp.sum(jnp.where(mine, scores, 0.0), axis=1, keepdims=True)
    factor = routed_scale * own / total

    for at in range(0, inner_width, inner_step):
        part = slice(at, at + inner_step)
        gate_part = jnp.dot(rows_ref[:, :width], gate_ref[:, part], preferred_element_type=jnp.float32)
        up_part = jnp.dot(rows_ref[:, :width], up_ref[:, part], preferred_element_type=jnp.float32)
        hidden = gate_part / (1.0 + jnp.exp(-gate_part)) * up_part * factor
        hidden_ref[:, part] = hidden.astype(jnp.bfloat16)
    slots = jnp.dot(picks, hidden_ref[...], preferred_element_type=jnp.float32).astype(jnp.bfloat16)

    blocks = total_rows // group
    row_in_tile = lax.broadcasted_iota(jnp.int32, (blocks, group, lanes), 1)
    tile = 0
    for at in range(0, width, outer_step):
        if copies:
            copies.pop(0).wait()
        part = slice(at, at + outer_step)
        y_ref[:, part] = jnp.dot(slots, down_ref[:, part], preferred_element_type=jnp.float32)
        while tile < tile_count(capacity, width) and chunks_in_tile(tile, capacity, width)[-1] < (at + outer_step) // lanes:
            packed = jnp.zeros((blocks, group, lanes), jnp.float32)
            for chunk in chunks_in_tile(tile, capacity, width):
                shift = chunk * capacity - group * tile
                piece = y_ref[:, chunk * lanes : (chunk + 1) * lanes].reshape(blocks, group, lanes)
                if shift % group:
                    piece = pltpu.roll(piece, shift % group, 1)
                packed = jnp.where((row_in_tile >= shift) & (row_in_tile < shift + capacity), piece, packed)
            out_ref[:, tile * lanes : (tile + 1) * lanes] = packed.reshape(total_rows, lanes).astype(jnp.bfloat16)
            tile += 1


def expert_shares(moment, micro_count, top_count, row_count, capacity, place, rows, ids, weights):
    total_rows = rows.shape[0]
    *held, down = weights
    inner_width, width = down.shape
    out_shape = [jax.ShapeDtypeStruct((total_rows, lanes * tile_count(capacity, width)), jnp.bfloat16)]
    scratch = [pltpu.VMEM((total_rows, inner_width), jnp.bfloat16), pltpu.VMEM((total_rows, width), jnp.float32)]
    if moment == 0:
        down = hbm(down)
        out_shape.append(jax.ShapeDtypeStruct(down.shape, down.dtype))
        scratch.append(pltpu.SemaphoreType.DMA((width // 512,)))
    shares, *new_down = pl.pallas_call(
        functools.partial(expert_kernel, moment, micro_count, top_count, row_count, capacity),
        out_shape=out_shape,
        in_specs=[in_vmem] * 6 + [in_hbm if moment == 0 else in_vmem],
        out_specs=[in_vmem] * len(out_shape),
        scratch_shapes=scratch,
        compiler_params=pltpu.CompilerParams(vmem_limit_bytes=10 * 1024 * 1024),
        cost_estimate=pl.CostEstimate(
            flops=6 * total_rows * width * inner_width, bytes_accessed=6 * width * inner_width, transcendentals=0
        ),
    )(place, rows, ids, *held, down)
    return shares, (*held, *(new_down or (down,)))


def sum_kernel(moment, capacity, own_section, place_ref, returned_ref, ids_ref, hidden_ref, *rest):
    *kept, out_ref = rest
    micro_count, row_count, top_count = ids_ref.shape
    width = hidden_ref.shape[1]
    total = returned_ref.shape[0]
    micro = micro_at(moment, micro_count, place_ref)
    lane_at = lax.broadcasted_iota(jnp.int32, (row_count, total), 1)
    row_at = lax.broadcasted_iota(jnp.int32, (row_count, total), 0)
    ids = ids_ref[0]
    for m in range(1, micro_count):
        ids = jnp.where(micro == m, ids_ref[m], ids)
    member = jnp.zeros((row_count, total), jnp.float32)
    for k in range(top_count):
        member = jnp.where(ids[:, k : k + 1] == lane_at // group, 1.0, member)
    slot = jnp.zeros((row_count, total), jnp.float32)
    for i in range(row_count - 1):
        slot = slot + jnp.where(row_at > i, member[i : i + 1, :], 0.0)
    slot = jnp.where(member > 0.5, slot, -1.0).astype(jnp.int32)
    sums = {}
    for tile in range(tile_count(capacity, width)):
        picks = []
        for chunk in chunks_in_tile(tile, capacity, width):
            wanted = lane_at % group + (group * tile - chunk * capacity)
            picks.append(jnp.where((slot == wanted) & (wanted >= 0) & (wanted < capacity), 1.0, 0.0))
        shares = returned_ref[:, tile * lanes : (tile + 1) * lanes]
        found = jnp.dot(jnp.concatenate(picks, axis=0).astype(jnp.bfloat16), shares, preferred_element_type=jnp.float32)
        for i, chunk in enumerate(chunks_in_tile(tile, capacity, width)):
            piece = found[i * row_count : (i + 1) * row_count]
            sums[chunk] = sums[chunk] + piece if chunk in sums else piece
    for chunk, branch in sums.items():
        part = slice(chunk * lanes, (chunk + 1) * lanes)
        result = (hidden_ref[:, part].astype(jnp.float32) + branch).astype(jnp.bfloat16)
        if kept:
            result = jnp.where(section_of(place_ref) == own_section, result, kept[0][:, part])
        out_ref[:, part] = result


def add_shares(moment, capacity, own_section, place, returned, ids, hidden, *kept):
    return pl.pallas_call(
        functools.partial(sum_kernel, moment, capacity, own_section),
        out_shape=jax.ShapeDtypeStruct(hidden.shape, jnp.bfloat16),
        in_specs=[in_vmem] * (4 + len(kept)),
        out_specs=in_vmem,
        compiler_params=pltpu.CompilerParams(vmem_limit_bytes=6 * 1024 * 1024),
    )(place, returned, ids, hidden, *kept)


def per_device(tokens, norm_gain, router, w_gate, w_up, w_down, expert_ids):
    sections = lax.axis_size("section")
    section_index = lax.axis_index("section")
    expert_count = lax.axis_size("expert")
    owner = lax.axis_index("expert")
    micro_count = expert_ids.shape[1]
    row_count = tokens.shape[1]
    width = tokens.shape[2]
    top_count = expert_ids.shape[3]
    capacity = min(row_count, max(2, 5 * row_count * top_count // (4 * expert_count)))
    router_rows = jnp.transpose(router[0])
    gate, up, down = (w[0, 0] for w in (w_gate, w_up, w_down))
    own_ids = expert_ids[0]
    inner = expert_count // outer_size
    same_outer = [[o * inner + i for i in range(inner)] for o in range(outer_size)]

    def sent(rows, route, shift):
        pairs = [
            (a * expert_count + e, b * expert_count + (e + shift * inner) % expert_count)
            for a, b in route
            for e in range(expert_count)
        ]
        return lax.ppermute(rows, ("section", "expert"), pairs)

    place = jnp.where(jnp.arange(lanes, dtype=jnp.int32)[None] == 0, owner, section_index).astype(jnp.int32)
    incoming = tokens[0]
    mixed = ids = None
    final = sections - 1
    total_moments = sections + micro_count - 1
    for moment in range(total_moments):
        if moment == 0:
            packed, place = first_norm(place, incoming, norm_gain, own_ids)
            stay = [(s, s) for s in range(sections)]
            blocks = [packed] + [sent(packed, stay, k) for k in range(1, outer_size)]
            place, held = hold(place, (router_rows, gate, up))
            weights = (*held, down)
            (rows,) = in_order(inner, place, blocks)
        else:
            rows, incoming = in_order(inner, place, blocks, norm_gain)
        rows = lax.all_gather(rows, "expert", axis=0, tiled=True, axis_index_groups=same_outer)
        ids = rows if ids is None else ids
        shares, weights = expert_shares(moment, micro_count, top_count, row_count, capacity, place, rows, ids, weights)
        returned = lax.all_to_all(
            shares.reshape(expert_count, group, shares.shape[1]), "expert", split_axis=0, concat_axis=0, tiled=True
        ).reshape(shares.shape)
        route = [(s, s + 1) for s in range(sections - 1)]
        own_section, kept, waiting = 0, (), []
        entering, finished = moment + 1, moment - final
        if finished == micro_count - 1:
            own_section, kept = final, () if mixed is None else (mixed,)
        elif entering == final and sections == 2:
            kept = (tokens[0],)
            route.append((final, 0))
        elif entering < micro_count:
            waiting = [sent(tokens[0], [(entering, 0)], k) for k in range(outer_size)]
        result = add_shares(moment, capacity, own_section, place, returned, own_ids, incoming, *kept)
        if finished == micro_count - 1:
            mixed = result
            break
        own_route = route + [(final, 0)] if finished == 0 else route
        blocks = [sent(result, own_route if k == 0 else route, k) for k in range(outer_size)] + waiting
        if finished == 0:
            mixed = blocks[0]
        elif finished > 0:
            mixed = jnp.where(section_index == finished, sent(result, [(final, finished)], 0), mixed)
    return mixed[None]


def solution(mesh):
    placed = (
        P("section", "expert", None),
        P("section", None),
        P("section", None, None),
        P("section", "expert", None, None),
        P("section", "expert", None, None),
        P("section", "expert", None, None),
        P("section", None, "expert", None),
    )
    return jax.shard_map(
        per_device,
        mesh=mesh,
        in_specs=placed,
        out_specs=P("section", "expert", None),
        check_vma=False,
    )
```

```python
import functools

import jax
import jax.numpy as jnp
from jax import lax
from jax.experimental import pallas as pl
from jax.experimental.pallas import tpu as pltpu
from jax.sharding import PartitionSpec as P

epsilon = 1e-06
routed_scale = 2.5
lanes = 128
outer_size = 4
cores = 2
in_vmem = pl.BlockSpec(memory_space=pltpu.VMEM)
in_hbm = pl.BlockSpec(memory_space=pltpu.HBM)


def hbm(array):
    return pltpu.with_memory_space_constraint(array, pltpu.HBM)


def owner_of(place_ref):
    return place_ref[0:1, 0:1]


def section_of(place_ref):
    return place_ref[0:1, 1:2]


def micro_at(moment, micro_count, place_ref):
    return jnp.minimum(jnp.maximum(moment - section_of(place_ref), 0), micro_count - 1)


def normalize(values, gain):
    inverse_rms = lax.rsqrt(jnp.mean(values * values, axis=-1, keepdims=True) + epsilon)
    return values * inverse_rms * gain


def start_all(copies):
    for copy in copies:
        copy.start()


def wait_all(copies):
    for copy in copies:
        copy.wait()


def first_norm_kernel(place_ref, tokens_hbm, gain_hbm, ids_hbm, out_ref, place_out, tokens_ref, gain_ref, ids_ref, sems):
    pairs = ((tokens_hbm, tokens_ref), (gain_hbm, gain_ref), (ids_hbm, ids_ref))
    copies = [pltpu.make_async_copy(source, target, sems.at[i]) for i, (source, target) in enumerate(pairs)]
    start_all(copies)
    place_out[...] = place_ref[...]
    wait_all(copies)
    row_count, width = tokens_ref.shape
    out_ref[:, :width] = normalize(tokens_ref[...].astype(jnp.float32), gain_ref[...].astype(jnp.float32)).astype(jnp.bfloat16)
    micro_count, _, top_count = ids_ref.shape
    lane_at = lax.broadcasted_iota(jnp.int32, (row_count, lanes), 1)
    named = jnp.zeros((row_count, lanes), jnp.float32)
    for m in range(micro_count):
        choices = ids_ref[m].astype(jnp.float32)
        for k in range(top_count):
            named = jnp.where(lane_at == m * top_count + k, choices[:, k : k + 1], named)
    out_ref[:, width:] = named.astype(jnp.bfloat16)


def first_norm(place, tokens, gain, ids):
    return pl.pallas_call(
        first_norm_kernel,
        out_shape=[
            jax.ShapeDtypeStruct((tokens.shape[0], tokens.shape[1] + lanes), jnp.bfloat16),
            jax.ShapeDtypeStruct(place.shape, place.dtype),
        ],
        in_specs=[in_vmem] + [in_hbm] * 3,
        out_specs=[in_vmem] * 2,
        scratch_shapes=[pltpu.VMEM(x.shape, x.dtype) for x in (tokens, gain, ids)] + [pltpu.SemaphoreType.DMA((3,))],
        compiler_params=pltpu.CompilerParams(vmem_limit_bytes=4 * 1024 * 1024),
    )(place, hbm(tokens), hbm(gain), hbm(ids))


def hold_kernel(place_ref, *refs):
    count = (len(refs) - 2) // 2
    sources, place_out, targets, sems = refs[:count], refs[count], refs[count + 1 : -1], refs[-1]
    copies = [pltpu.make_async_copy(source, target, sems.at[i]) for i, (source, target) in enumerate(zip(sources, targets))]
    start_all(copies)
    place_out[...] = place_ref[...]
    wait_all(copies)


def hold(place, arrays):
    place, *held = pl.pallas_call(
        hold_kernel,
        out_shape=[jax.ShapeDtypeStruct(x.shape, x.dtype) for x in (place, *arrays)],
        in_specs=[in_vmem] + [in_hbm] * len(arrays),
        out_specs=[in_vmem] * (1 + len(arrays)),
        scratch_shapes=[pltpu.SemaphoreType.DMA((len(arrays),))],
        compiler_params=pltpu.CompilerParams(vmem_limit_bytes=1024 * 1024),
        cost_estimate=pl.CostEstimate(
            flops=0, bytes_accessed=2 * sum(x.size * x.dtype.itemsize for x in arrays), transcendentals=0
        ),
    )(place, *[hbm(x) for x in arrays])
    return place, held


def order_kernel(norm, inner, place_ref, *refs):
    if norm:
        *refs, gain_ref, out_ref, own_out = refs
    else:
        *refs, out_ref = refs
    outer = outer_size
    blocks = [ref[...].astype(jnp.float32) for ref in refs[:outer]]
    if len(refs) > outer:
        waiting = [ref[...].astype(jnp.float32) for ref in refs[outer:]]
        blocks = [jnp.where(section_of(place_ref) == 0, w, b) for w, b in zip(waiting, blocks)]
    if norm:
        own_out[...] = blocks[0].astype(jnp.bfloat16)
        blocks = [normalize(b, gain_ref[...].astype(jnp.float32)) for b in blocks]
    owner = owner_of(place_ref)
    here = [(owner >= o * inner) & (owner < (o + 1) * inner) for o in range(outer)]
    ordered = []
    for at in range(outer):
        block = blocks[0]
        for k in range(1, outer):
            block = jnp.where(here[(at + k) % outer], blocks[k], block)
        ordered.append(block)
    out_ref[...] = jnp.concatenate(ordered, axis=0).astype(jnp.bfloat16)


def in_order(inner, place, blocks, *gain):
    row_count, width = blocks[0].shape
    out_shape = [jax.ShapeDtypeStruct((outer_size * row_count, width), jnp.bfloat16)]
    if gain:
        out_shape.append(jax.ShapeDtypeStruct((row_count, width), jnp.bfloat16))
    return pl.pallas_call(
        functools.partial(order_kernel, bool(gain), inner),
        out_shape=out_shape,
        in_specs=[in_vmem] * (1 + len(blocks) + len(gain)),
        out_specs=[in_vmem] * len(out_shape),
        compiler_params=pltpu.CompilerParams(vmem_limit_bytes=6 * 1024 * 1024),
    )(place, *blocks, *gain)


def expert_kernel(
    moment, micro_count, top_count, row_count, capacity,
    place_ref, rows_ref, ids_ref, router_ref, gate_ref, up_ref, down_ref, own_ref, other_ref, *rest,
):
    inner_width, width = down_ref.shape
    inner_step, outer_step = 512, 512
    copies = []
    if moment == 0:
        down_hbm, (down_ref, *rest, sems) = down_ref, rest
        for i, at in enumerate(range(0, width, outer_step)):
            part = (slice(None), pl.ds(at, outer_step))
            copies.append(pltpu.make_async_copy(down_hbm.at[part], down_ref.at[part], sems.at[i]))
        start_all(copies)
    (hidden_ref,) = rest
    total_rows = rows_ref.shape[0]
    expert_count = router_ref.shape[0]
    inner = expert_count // outer_size

    owner, micro = owner_of(place_ref), micro_at(moment, micro_count, place_ref)
    ids = ids_ref[:, ids_ref.shape[1] - lanes :].astype(jnp.float32)
    names = lax.broadcasted_iota(jnp.int32, (total_rows, expert_count), 1).astype(jnp.float32)
    member = jnp.zeros((total_rows, expert_count), jnp.float32)
    for k in range(top_count):
        choice = ids[:, k : k + 1]
        for m in range(1, micro_count):
            at = m * top_count + k
            choice = jnp.where(micro == m, ids[:, at : at + 1], choice)
        member = jnp.where(choice == names, 1.0, member)
    mine = names == owner.astype(jnp.float32)
    row_at = lax.broadcasted_iota(jnp.int32, (total_rows, total_rows), 0)
    column_at = lax.broadcasted_iota(jnp.int32, (total_rows, total_rows), 1)
    block_at = row_at // row_count
    before = (column_at < row_at) & (column_at // row_count == block_at)
    named = jnp.where(mine, member, 0.0)
    earlier = jnp.dot(
        jnp.where(before, 1.0, 0.0).astype(jnp.bfloat16), named.astype(jnp.bfloat16), preferred_element_type=jnp.float32
    )
    slot = jnp.sum(jnp.where(mine, earlier, 0.0), axis=1, keepdims=True)
    named = jnp.sum(named, axis=1, keepdims=True)
    kept = (named > 0.5) & (slot < capacity - 0.5)
    device_at = block_at % outer_size * inner + block_at // outer_size
    other_core = device_at % cores != lax.rem(owner, cores)
    goal_at = device_at // cores + jnp.where(other_core, total_rows // row_count // cores, 0)
    picks = (column_at // row_count == goal_at) & (column_at % row_count == row_at % row_count) & kept
    picks = jnp.transpose(jnp.where(picks, 1.0, 0.0)).astype(jnp.bfloat16)

    logits = lax.dot_general(
        rows_ref[:, :width], router_ref[...], (((1,), (1,)), ((), ())), preferred_element_type=jnp.float32
    )
    scores = jax.nn.sigmoid(logits)
    total = jnp.sum(jnp.where(member > 0.5, scores, 0.0), axis=1, keepdims=True)
    own = jnp.sum(jnp.where(mine, scores, 0.0), axis=1, keepdims=True)
    factor = routed_scale * own / total

    for at in range(0, inner_width, inner_step):
        part = slice(at, at + inner_step)
        gate_part = jnp.dot(rows_ref[:, :width], gate_ref[:, part], preferred_element_type=jnp.float32)
        up_part = jnp.dot(rows_ref[:, :width], up_ref[:, part], preferred_element_type=jnp.float32)
        hidden = gate_part / (1.0 + jnp.exp(-gate_part)) * up_part * factor
        hidden_ref[:, part] = hidden.astype(jnp.bfloat16)
    hidden = jnp.dot(picks, hidden_ref[...], preferred_element_type=jnp.float32).astype(jnp.bfloat16)
    half = total_rows // cores
    for at in range(0, width, outer_step):
        if copies:
            copies.pop(0).wait()
        part = slice(at, at + outer_step)
        share = jnp.dot(hidden, down_ref[:, part], preferred_element_type=jnp.float32)
        own_ref[:, part] = share[:half]
        other_ref[:, part] = share[half:].astype(jnp.bfloat16)


def expert_shares(moment, micro_count, top_count, row_count, capacity, place, rows, ids, weights):
    total_rows = rows.shape[0]
    *held, down = weights
    inner_width, width = down.shape
    half = (total_rows // cores, width)
    out_shape = [jax.ShapeDtypeStruct(half, jnp.float32), jax.ShapeDtypeStruct(half, jnp.bfloat16)]
    scratch = [pltpu.VMEM((total_rows, inner_width), jnp.bfloat16)]
    if moment == 0:
        down = hbm(down)
        out_shape.append(jax.ShapeDtypeStruct(down.shape, down.dtype))
        scratch.append(pltpu.SemaphoreType.DMA((width // 512,)))
    own, other, *new_down = pl.pallas_call(
        functools.partial(expert_kernel, moment, micro_count, top_count, row_count, capacity),
        out_shape=out_shape,
        in_specs=[in_vmem] * 6 + [in_hbm if moment == 0 else in_vmem],
        out_specs=[in_vmem] * len(out_shape),
        scratch_shapes=scratch,
        compiler_params=pltpu.CompilerParams(vmem_limit_bytes=10 * 1024 * 1024),
        cost_estimate=pl.CostEstimate(
            flops=6 * total_rows * width * inner_width, bytes_accessed=6 * width * inner_width, transcendentals=0
        ),
    )(place, rows, ids, *held, down)
    return own, other, (*held, *(new_down or (down,)))


def chip_kernel(own_ref, other_ref, out_ref):
    out_ref[...] = (own_ref[...] + other_ref[...].astype(jnp.float32)).astype(jnp.bfloat16)


def chip_shares(own, other):
    return pl.pallas_call(
        chip_kernel,
        out_shape=jax.ShapeDtypeStruct(other.shape, jnp.bfloat16),
        in_specs=[in_vmem] * 2,
        out_specs=in_vmem,
        compiler_params=pltpu.CompilerParams(vmem_limit_bytes=6 * 1024 * 1024),
    )(own, other)


def sum_kernel(own_section, place_ref, returned_ref, hidden_ref, *rest):
    *kept, out_ref = rest
    row_count = hidden_ref.shape[0]
    result = hidden_ref[...].astype(jnp.float32)
    shares = returned_ref[...].astype(jnp.float32)
    for at in range(0, shares.shape[0], row_count):
        result = result + shares[at : at + row_count]
    result = result.astype(jnp.bfloat16)
    if kept:
        result = jnp.where(section_of(place_ref) == own_section, result, kept[0][...])
    out_ref[...] = result


def add_shares(own_section, place, returned, hidden, *kept):
    return pl.pallas_call(
        functools.partial(sum_kernel, own_section),
        out_shape=jax.ShapeDtypeStruct(hidden.shape, jnp.bfloat16),
        in_specs=[in_vmem] * (3 + len(kept)),
        out_specs=in_vmem,
        compiler_params=pltpu.CompilerParams(vmem_limit_bytes=6 * 1024 * 1024),
    )(place, returned, hidden, *kept)


def per_device(tokens, norm_gain, router, w_gate, w_up, w_down, expert_ids):
    sections = lax.axis_size("section")
    section_index = lax.axis_index("section")
    expert_count = lax.axis_size("expert")
    owner = lax.axis_index("expert")
    micro_count = expert_ids.shape[1]
    row_count = tokens.shape[1]
    width = tokens.shape[2]
    top_count = expert_ids.shape[3]
    capacity = min(row_count, max(2, 5 * row_count * top_count // (4 * expert_count)))
    router_rows = jnp.transpose(router[0])
    gate, up, down = (w[0, 0] for w in (w_gate, w_up, w_down))
    own_ids = expert_ids[0]
    inner = expert_count // outer_size
    same_core = [list(range(c, expert_count, cores)) for c in range(cores)]
    swap = [(e, e + 1 - 2 * (e % cores)) for e in range(expert_count)]
    same_outer = [[o * inner + i for i in range(inner)] for o in range(outer_size)]

    def sent(rows, route, shift):
        pairs = [
            (a * expert_count + e, b * expert_count + (e + shift * inner) % expert_count)
            for a, b in route
            for e in range(expert_count)
        ]
        return lax.ppermute(rows, ("section", "expert"), pairs)

    place = jnp.where(jnp.arange(lanes, dtype=jnp.int32)[None] == 0, owner, section_index).astype(jnp.int32)
    incoming = tokens[0]
    mixed = ids = None
    final = sections - 1
    total_moments = sections + micro_count - 1
    for moment in range(total_moments):
        if moment == 0:
            packed, place = first_norm(place, incoming, norm_gain, own_ids)
            stay = [(s, s) for s in range(sections)]
            blocks = [packed] + [sent(packed, stay, k) for k in range(1, outer_size)]
            place, held = hold(place, (router_rows, gate, up))
            weights = (*held, down)
            (rows,) = in_order(inner, place, blocks)
        else:
            rows, incoming = in_order(inner, place, blocks, norm_gain)
        rows = lax.all_gather(rows, "expert", axis=0, tiled=True, axis_index_groups=same_outer)
        ids = rows if ids is None else ids
        own, other, weights = expert_shares(moment, micro_count, top_count, row_count, capacity, place, rows, ids, weights)
        shares = chip_shares(own, lax.ppermute(other, "expert", swap))
        returned = lax.all_to_all(
            shares.reshape(-1, row_count, width), "expert", split_axis=0, concat_axis=0, tiled=True, axis_index_groups=same_core
        ).reshape(shares.shape)
        route = [(s, s + 1) for s in range(sections - 1)]
        own_section, kept, waiting = 0, (), []
        entering, finished = moment + 1, moment - final
        if finished == micro_count - 1:
            own_section, kept = final, () if mixed is None else (mixed,)
        elif entering == final and sections == 2:
            kept = (tokens[0],)
            route.append((final, 0))
        elif entering < micro_count:
            waiting = [sent(tokens[0], [(entering, 0)], k) for k in range(outer_size)]
        result = add_shares(own_section, place, returned, incoming, *kept)
        if finished == micro_count - 1:
            mixed = result
            break
        own_route = route + [(final, 0)] if finished == 0 else route
        blocks = [sent(result, own_route if k == 0 else route, k) for k in range(outer_size)] + waiting
        if finished == 0:
            mixed = blocks[0]
        elif finished > 0:
            mixed = jnp.where(section_index == finished, sent(result, [(final, finished)], 0), mixed)
    return mixed[None]


def solution(mesh):
    placed = (
        P("section", "expert", None),
        P("section", None),
        P("section", None, None),
        P("section", "expert", None, None),
        P("section", "expert", None, None),
        P("section", "expert", None, None),
        P("section", None, "expert", None),
    )
    return jax.shard_map(
        per_device,
        mesh=mesh,
        in_specs=placed,
        out_specs=P("section", "expert", None),
        check_vma=False,
    )
```

```python
import functools

import jax
import jax.numpy as jnp
from jax import lax
from jax.experimental import pallas as pl
from jax.experimental.pallas import tpu as pltpu
from jax.sharding import PartitionSpec as P

epsilon = 1e-06
routed_scale = 2.5
lanes = 128
outer_size = 4
cores = 2
in_vmem = pl.BlockSpec(memory_space=pltpu.VMEM)
in_hbm = pl.BlockSpec(memory_space=pltpu.HBM)


def hbm(array):
    return pltpu.with_memory_space_constraint(array, pltpu.HBM)


def owner_of(place_ref):
    return place_ref[0:1, 0:1]


def section_of(place_ref):
    return place_ref[0:1, 1:2]


def micro_at(moment, micro_count, place_ref):
    return jnp.minimum(jnp.maximum(moment - section_of(place_ref), 0), micro_count - 1)


def normalize(values, gain):
    inverse_rms = lax.rsqrt(jnp.mean(values * values, axis=-1, keepdims=True) + epsilon)
    return values * inverse_rms * gain


def start_all(copies):
    for copy in copies:
        copy.start()


def wait_all(copies):
    for copy in copies:
        copy.wait()


def first_norm_kernel(place_ref, tokens_hbm, gain_hbm, ids_hbm, out_ref, place_out, tokens_ref, gain_ref, ids_ref, sems):
    pairs = ((tokens_hbm, tokens_ref), (gain_hbm, gain_ref), (ids_hbm, ids_ref))
    copies = [pltpu.make_async_copy(source, target, sems.at[i]) for i, (source, target) in enumerate(pairs)]
    start_all(copies)
    place_out[...] = place_ref[...]
    wait_all(copies)
    row_count, width = tokens_ref.shape
    out_ref[:, :width] = normalize(tokens_ref[...].astype(jnp.float32), gain_ref[...].astype(jnp.float32)).astype(jnp.bfloat16)
    micro_count, _, top_count = ids_ref.shape
    lane_at = lax.broadcasted_iota(jnp.int32, (row_count, lanes), 1)
    named = jnp.zeros((row_count, lanes), jnp.float32)
    for m in range(micro_count):
        choices = ids_ref[m].astype(jnp.float32)
        for k in range(top_count):
            named = jnp.where(lane_at == m * top_count + k, choices[:, k : k + 1], named)
    out_ref[:, width:] = named.astype(jnp.bfloat16)


def first_norm(place, tokens, gain, ids):
    return pl.pallas_call(
        first_norm_kernel,
        out_shape=[
            jax.ShapeDtypeStruct((tokens.shape[0], tokens.shape[1] + lanes), jnp.bfloat16),
            jax.ShapeDtypeStruct(place.shape, place.dtype),
        ],
        in_specs=[in_vmem] + [in_hbm] * 3,
        out_specs=[in_vmem] * 2,
        scratch_shapes=[pltpu.VMEM(x.shape, x.dtype) for x in (tokens, gain, ids)] + [pltpu.SemaphoreType.DMA((3,))],
        compiler_params=pltpu.CompilerParams(vmem_limit_bytes=4 * 1024 * 1024),
    )(place, hbm(tokens), hbm(gain), hbm(ids))


def hold_kernel(place_ref, *refs):
    count = (len(refs) - 2) // 2
    sources, place_out, targets, sems = refs[:count], refs[count], refs[count + 1 : -1], refs[-1]
    copies = [pltpu.make_async_copy(source, target, sems.at[i]) for i, (source, target) in enumerate(zip(sources, targets))]
    start_all(copies)
    place_out[...] = place_ref[...]
    wait_all(copies)


def hold(place, arrays):
    place, *held = pl.pallas_call(
        hold_kernel,
        out_shape=[jax.ShapeDtypeStruct(x.shape, x.dtype) for x in (place, *arrays)],
        in_specs=[in_vmem] + [in_hbm] * len(arrays),
        out_specs=[in_vmem] * (1 + len(arrays)),
        scratch_shapes=[pltpu.SemaphoreType.DMA((len(arrays),))],
        compiler_params=pltpu.CompilerParams(vmem_limit_bytes=1024 * 1024),
        cost_estimate=pl.CostEstimate(
            flops=0, bytes_accessed=2 * sum(x.size * x.dtype.itemsize for x in arrays), transcendentals=0
        ),
    )(place, *[hbm(x) for x in arrays])
    return place, held


def order_kernel(norm, inner, place_ref, *refs):
    if norm:
        *refs, gain_ref, out_ref, own_out = refs
    else:
        *refs, out_ref = refs
    outer = outer_size
    blocks = [ref[...].astype(jnp.float32) for ref in refs[:outer]]
    if len(refs) > outer:
        waiting = [ref[...].astype(jnp.float32) for ref in refs[outer:]]
        blocks = [jnp.where(section_of(place_ref) == 0, w, b) for w, b in zip(waiting, blocks)]
    if norm:
        own_out[...] = blocks[0].astype(jnp.bfloat16)
        blocks = [normalize(b, gain_ref[...].astype(jnp.float32)) for b in blocks]
    owner = owner_of(place_ref)
    here = [(owner >= o * inner) & (owner < (o + 1) * inner) for o in range(outer)]
    ordered = []
    for at in range(outer):
        block = blocks[0]
        for k in range(1, outer):
            block = jnp.where(here[(at + k) % outer], blocks[k], block)
        ordered.append(block)
    out_ref[...] = jnp.concatenate(ordered, axis=0).astype(jnp.bfloat16)


def in_order(inner, place, blocks, *gain):
    row_count, width = blocks[0].shape
    out_shape = [jax.ShapeDtypeStruct((outer_size * row_count, width), jnp.bfloat16)]
    if gain:
        out_shape.append(jax.ShapeDtypeStruct((row_count, width), jnp.bfloat16))
    return pl.pallas_call(
        functools.partial(order_kernel, bool(gain), inner),
        out_shape=out_shape,
        in_specs=[in_vmem] * (1 + len(blocks) + len(gain)),
        out_specs=[in_vmem] * len(out_shape),
        compiler_params=pltpu.CompilerParams(vmem_limit_bytes=6 * 1024 * 1024),
    )(place, *blocks, *gain)


def expert_kernel(moment, micro_count, top_count, row_count, capacity, place_ref, *refs):
    count = (len(refs) - 6) // 3
    rows_refs, ids_refs, (router_ref, gate_ref, up_ref, down_ref), out_refs = (
        refs[:count], refs[count : 2 * count], refs[2 * count : 2 * count + 4], refs[2 * count + 4 : -2]
    )
    rows_ref, hidden_ref = refs[-2:]
    inner_width, width = down_ref.shape
    inner_step, outer_step = 512, 512
    total_rows = rows_ref.shape[0]
    part_rows = total_rows // count
    expert_count = router_ref.shape[0]
    for i, ref in enumerate(rows_refs):
        rows_ref[i * part_rows : (i + 1) * part_rows, :] = ref[:, :width]

    owner, micro = owner_of(place_ref), micro_at(moment, micro_count, place_ref)
    ids = jnp.concatenate([ref[:, ref.shape[1] - lanes :].astype(jnp.float32) for ref in ids_refs], axis=0)
    names = lax.broadcasted_iota(jnp.int32, (total_rows, expert_count), 1).astype(jnp.float32)
    member = jnp.zeros((total_rows, expert_count), jnp.float32)
    for k in range(top_count):
        choice = ids[:, k : k + 1]
        for m in range(1, micro_count):
            at = m * top_count + k
            choice = jnp.where(micro == m, ids[:, at : at + 1], choice)
        member = jnp.where(choice == names, 1.0, member)
    mine = names == owner.astype(jnp.float32)
    row_at = lax.broadcasted_iota(jnp.int32, (total_rows, total_rows), 0)
    column_at = lax.broadcasted_iota(jnp.int32, (total_rows, total_rows), 1)
    before = (column_at < row_at) & (column_at // row_count == row_at // row_count)
    named = jnp.where(mine, member, 0.0)
    earlier = jnp.dot(
        jnp.where(before, 1.0, 0.0).astype(jnp.bfloat16), named.astype(jnp.bfloat16), preferred_element_type=jnp.float32
    )
    slot = jnp.sum(jnp.where(mine, earlier, 0.0), axis=1, keepdims=True)
    kept = (jnp.sum(named, axis=1, keepdims=True) > 0.5) & (slot < capacity - 0.5)
    logits = lax.dot_general(rows_ref[...], router_ref[...], (((1,), (1,)), ((), ())), preferred_element_type=jnp.float32)
    scores = jax.nn.sigmoid(logits)
    total = jnp.sum(jnp.where(member > 0.5, scores, 0.0), axis=1, keepdims=True)
    own = jnp.sum(jnp.where(mine, scores, 0.0), axis=1, keepdims=True)
    factor = jnp.where(kept, routed_scale * own / total, 0.0)

    for at in range(0, inner_width, inner_step):
        part = slice(at, at + inner_step)
        gate_part = jnp.dot(rows_ref[...], gate_ref[:, part], preferred_element_type=jnp.float32)
        up_part = jnp.dot(rows_ref[...], up_ref[:, part], preferred_element_type=jnp.float32)
        hidden = gate_part / (1.0 + jnp.exp(-gate_part)) * up_part
        hidden_ref[:, part] = jnp.where(kept, hidden * factor, 0.0).astype(jnp.bfloat16)
    hidden = hidden_ref[...]
    for at in range(0, width, outer_step):
        part = slice(at, at + outer_step)
        share = jnp.dot(hidden, down_ref[:, part], preferred_element_type=jnp.float32)
        for i, out_ref in enumerate(out_refs):
            out_ref[:, part] = share[i * part_rows : (i + 1) * part_rows].astype(out_ref.dtype)


def expert_shares(moment, micro_count, top_count, row_count, capacity, place, rows, ids, weights):
    part_rows = rows[0].shape[0]
    inner_width, width = weights[3].shape
    total_rows = len(rows) * part_rows
    return pl.pallas_call(
        functools.partial(expert_kernel, moment, micro_count, top_count, row_count, capacity),
        out_shape=[
            jax.ShapeDtypeStruct((part_rows, width), jnp.bfloat16 if i % cores else jnp.float32) for i in range(len(rows))
        ],
        in_specs=[in_vmem] * (1 + 2 * len(rows) + 4),
        out_specs=[in_vmem] * len(rows),
        scratch_shapes=[pltpu.VMEM((total_rows, width), jnp.bfloat16), pltpu.VMEM((total_rows, inner_width), jnp.bfloat16)],
        compiler_params=pltpu.CompilerParams(vmem_limit_bytes=10 * 1024 * 1024),
        cost_estimate=pl.CostEstimate(
            flops=6 * total_rows * width * inner_width, bytes_accessed=6 * width * inner_width, transcendentals=0
        ),
    )(place, *rows, *ids, *weights)


def chip_kernel(row_count, inner, place_ref, *refs):
    *refs, out_ref = refs
    places = inner // cores
    at_inner = lax.rem(owner_of(place_ref), inner)
    here = [(at_inner >= x * cores) & (at_inner < (x + 1) * cores) for x in range(places)]
    sums = [refs[2 * h][...] + refs[2 * h + 1][...].astype(jnp.float32) for h in range(places)]
    blocks = []
    for o in range(outer_size):
        block = slice(o * row_count, (o + 1) * row_count)
        for x in range(places):
            share = sums[0][block]
            for h in range(1, places):
                share = jnp.where(here[(x + h) % places], sums[h][block], share)
            blocks.append(share)
    out_ref[...] = jnp.concatenate(blocks, axis=0).astype(jnp.bfloat16)


def chip_shares(row_count, inner, place, shares):
    rows, width = shares[0].shape
    return pl.pallas_call(
        functools.partial(chip_kernel, row_count, inner),
        out_shape=jax.ShapeDtypeStruct((rows * len(shares) // cores, width), jnp.bfloat16),
        in_specs=[in_vmem] * (1 + len(shares)),
        out_specs=in_vmem,
        compiler_params=pltpu.CompilerParams(vmem_limit_bytes=8 * 1024 * 1024),
    )(place, *shares)


def sum_kernel(own_section, place_ref, returned_ref, hidden_ref, *rest):
    *kept, out_ref = rest
    row_count = hidden_ref.shape[0]
    result = hidden_ref[...].astype(jnp.float32)
    shares = returned_ref[...].astype(jnp.float32)
    for at in range(0, shares.shape[0], row_count):
        result = result + shares[at : at + row_count]
    result = result.astype(jnp.bfloat16)
    if kept:
        result = jnp.where(section_of(place_ref) == own_section, result, kept[0][...])
    out_ref[...] = result


def add_shares(own_section, place, returned, hidden, *kept):
    return pl.pallas_call(
        functools.partial(sum_kernel, own_section),
        out_shape=jax.ShapeDtypeStruct(hidden.shape, jnp.bfloat16),
        in_specs=[in_vmem] * (3 + len(kept)),
        out_specs=in_vmem,
        compiler_params=pltpu.CompilerParams(vmem_limit_bytes=6 * 1024 * 1024),
    )(place, returned, hidden, *kept)


def per_device(tokens, norm_gain, router, w_gate, w_up, w_down, expert_ids):
    sections = lax.axis_size("section")
    section_index = lax.axis_index("section")
    expert_count = lax.axis_size("expert")
    owner = lax.axis_index("expert")
    micro_count = expert_ids.shape[1]
    row_count = tokens.shape[1]
    width = tokens.shape[2]
    top_count = expert_ids.shape[3]
    capacity = min(row_count, max(2, 5 * row_count * top_count // (4 * expert_count)))
    router_rows = jnp.transpose(router[0])
    gate, up, down = (w[0, 0] for w in (w_gate, w_up, w_down))
    own_ids = expert_ids[0]
    inner = expert_count // outer_size
    same_core = [list(range(c, expert_count, cores)) for c in range(cores)]
    swap = [(e, e + 1 - 2 * (e % cores)) for e in range(expert_count)]

    def swapped(rows):
        return lax.ppermute(rows, "expert", swap)

    def along_x(rows, shift):
        pairs = [(e, e // inner * inner + (e + shift * cores) % inner) for e in range(expert_count)]
        return lax.ppermute(rows, "expert", pairs)

    def sent(rows, route, shift):
        pairs = [
            (a * expert_count + e, b * expert_count + (e + shift * inner) % expert_count)
            for a, b in route
            for e in range(expert_count)
        ]
        return lax.ppermute(rows, ("section", "expert"), pairs)

    place = jnp.where(jnp.arange(lanes, dtype=jnp.int32)[None] == 0, owner, section_index).astype(jnp.int32)
    incoming = tokens[0]
    mixed = ids = None
    final = sections - 1
    total_moments = sections + micro_count - 1
    for moment in range(total_moments):
        if moment == 0:
            packed, place = first_norm(place, incoming, norm_gain, own_ids)
            stay = [(s, s) for s in range(sections)]
            blocks = [packed] + [sent(packed, stay, k) for k in range(1, outer_size)]
            place, (router_held, gate_held) = hold(place, (router_rows, gate))
            (ordered,) = in_order(inner, place, blocks)
            ordered, place = lax.optimization_barrier((ordered, place))
        else:
            ordered, incoming = in_order(inner, place, blocks, norm_gain)
        rows = [ordered, swapped(ordered)]
        coming = [along_x(ordered, h) for h in range(1, inner // cores)]
        run = functools.partial(expert_shares, moment, micro_count, top_count, row_count, capacity)
        if moment == 0:
            place, (up_held, down_held) = hold(place, (up, down))
            weights = (router_held, gate_held, up_held, down_held)
            coming, place = lax.optimization_barrier((coming, place))
            ids = rows = rows + [r for row in coming for r in (row, swapped(row))]
            shares = list(run(place, rows, ids, weights))
        else:
            shares = list(run(place, rows, ids[:cores], weights))
            coming, shares[0] = lax.optimization_barrier((coming, shares[0]))
            for h, row in enumerate(coming, 1):
                shares += run(place, [row, swapped(row)], ids[h * cores : (h + 1) * cores], weights)
        shares = [swapped(share) if i % cores else share for i, share in enumerate(shares)]
        shares = chip_shares(row_count, inner, place, shares)
        returned = lax.all_to_all(
            shares.reshape(-1, row_count, width), "expert", split_axis=0, concat_axis=0, tiled=True, axis_index_groups=same_core
        ).reshape(shares.shape)
        route = [(s, s + 1) for s in range(sections - 1)]
        own_section, kept, waiting = 0, (), []
        entering, finished = moment + 1, moment - final
        if finished == micro_count - 1:
            own_section, kept = final, () if mixed is None else (mixed,)
        elif entering == final and sections == 2:
            kept = (tokens[0],)
            route.append((final, 0))
        elif entering < micro_count:
            waiting = [sent(tokens[0], [(entering, 0)], k) for k in range(outer_size)]
        result = add_shares(own_section, place, returned, incoming, *kept)
        if finished == micro_count - 1:
            mixed = result
            break
        own_route = route + [(final, 0)] if finished == 0 else route
        blocks = [sent(result, own_route if k == 0 else route, k) for k in range(outer_size)] + waiting
        if finished == 0:
            mixed = blocks[0]
        elif finished > 0:
            mixed = jnp.where(section_index == finished, sent(result, [(final, finished)], 0), mixed)
    return mixed[None]


def solution(mesh):
    placed = (
        P("section", "expert", None),
        P("section", None),
        P("section", None, None),
        P("section", "expert", None, None),
        P("section", "expert", None, None),
        P("section", "expert", None, None),
        P("section", None, "expert", None),
    )
    return jax.shard_map(
        per_device,
        mesh=mesh,
        in_specs=placed,
        out_specs=P("section", "expert", None),
        check_vma=False,
    )
```

```python
import functools

import jax
import jax.numpy as jnp
from jax import lax
from jax.experimental import pallas as pl
from jax.experimental.pallas import tpu as pltpu
from jax.sharding import PartitionSpec as P

epsilon = 1e-06
routed_scale = 2.5
lanes = 128
outer_size = 4
cores = 2
in_vmem = pl.BlockSpec(memory_space=pltpu.VMEM)
in_hbm = pl.BlockSpec(memory_space=pltpu.HBM)


def hbm(array):
    return pltpu.with_memory_space_constraint(array, pltpu.HBM)


def owner_of(place_ref):
    return place_ref[0:1, 0:1]


def section_of(place_ref):
    return place_ref[0:1, 1:2]


def micro_at(moment, micro_count, place_ref):
    return jnp.minimum(jnp.maximum(moment - section_of(place_ref), 0), micro_count - 1)


def normalize(values, gain):
    inverse_rms = lax.rsqrt(jnp.mean(values * values, axis=-1, keepdims=True) + epsilon)
    return values * inverse_rms * gain


def start_all(copies):
    for copy in copies:
        copy.start()


def wait_all(copies):
    for copy in copies:
        copy.wait()


def first_norm_kernel(place_ref, tokens_hbm, gain_hbm, ids_hbm, out_ref, place_out, tokens_ref, gain_ref, ids_ref, sems):
    pairs = ((tokens_hbm, tokens_ref), (gain_hbm, gain_ref), (ids_hbm, ids_ref))
    copies = [pltpu.make_async_copy(source, target, sems.at[i]) for i, (source, target) in enumerate(pairs)]
    start_all(copies)
    place_out[...] = place_ref[...]
    wait_all(copies)
    row_count, width = tokens_ref.shape
    out_ref[:, :width] = normalize(tokens_ref[...].astype(jnp.float32), gain_ref[...].astype(jnp.float32)).astype(jnp.bfloat16)
    micro_count, _, top_count = ids_ref.shape
    lane_at = lax.broadcasted_iota(jnp.int32, (row_count, lanes), 1)
    named = jnp.zeros((row_count, lanes), jnp.float32)
    for m in range(micro_count):
        choices = ids_ref[m].astype(jnp.float32)
        for k in range(top_count):
            named = jnp.where(lane_at == m * top_count + k, choices[:, k : k + 1], named)
    out_ref[:, width:] = named.astype(jnp.bfloat16)


def first_norm(place, tokens, gain, ids):
    return pl.pallas_call(
        first_norm_kernel,
        out_shape=[
            jax.ShapeDtypeStruct((tokens.shape[0], tokens.shape[1] + lanes), jnp.bfloat16),
            jax.ShapeDtypeStruct(place.shape, place.dtype),
        ],
        in_specs=[in_vmem] + [in_hbm] * 3,
        out_specs=[in_vmem] * 2,
        scratch_shapes=[pltpu.VMEM(x.shape, x.dtype) for x in (tokens, gain, ids)] + [pltpu.SemaphoreType.DMA((3,))],
        compiler_params=pltpu.CompilerParams(vmem_limit_bytes=4 * 1024 * 1024),
    )(place, hbm(tokens), hbm(gain), hbm(ids))


def hold_kernel(place_ref, *refs):
    count = (len(refs) - 2) // 2
    sources, place_out, targets, sems = refs[:count], refs[count], refs[count + 1 : -1], refs[-1]
    copies = [pltpu.make_async_copy(source, target, sems.at[i]) for i, (source, target) in enumerate(zip(sources, targets))]
    start_all(copies)
    place_out[...] = place_ref[...]
    wait_all(copies)


def hold(place, arrays):
    place, *held = pl.pallas_call(
        hold_kernel,
        out_shape=[jax.ShapeDtypeStruct(x.shape, x.dtype) for x in (place, *arrays)],
        in_specs=[in_vmem] + [in_hbm] * len(arrays),
        out_specs=[in_vmem] * (1 + len(arrays)),
        scratch_shapes=[pltpu.SemaphoreType.DMA((len(arrays),))],
        compiler_params=pltpu.CompilerParams(vmem_limit_bytes=1024 * 1024),
        cost_estimate=pl.CostEstimate(
            flops=0, bytes_accessed=2 * sum(x.size * x.dtype.itemsize for x in arrays), transcendentals=0
        ),
    )(place, *[hbm(x) for x in arrays])
    return place, held


def outer_is(place_ref, inner):
    owner = owner_of(place_ref)
    return [(owner >= o * inner) & (owner < (o + 1) * inner) for o in range(outer_size)]


def order_kernel(inner, place_ref, *refs):
    *refs, out_ref = refs
    blocks = [ref[...].astype(jnp.float32) for ref in refs]
    here = outer_is(place_ref, inner)
    ordered = []
    for at in range(outer_size):
        block = blocks[0]
        for k in range(1, outer_size):
            block = jnp.where(here[(at + k) % outer_size], blocks[k], block)
        ordered.append(block)
    out_ref[...] = jnp.concatenate(ordered, axis=0).astype(jnp.bfloat16)


def in_order(inner, place, blocks):
    row_count, width = blocks[0].shape
    return pl.pallas_call(
        functools.partial(order_kernel, inner),
        out_shape=jax.ShapeDtypeStruct((outer_size * row_count, width), jnp.bfloat16),
        in_specs=[in_vmem] * (1 + len(blocks)),
        out_specs=in_vmem,
        compiler_params=pltpu.CompilerParams(vmem_limit_bytes=6 * 1024 * 1024),
    )(place, *blocks)


def expert_kernel(moment, micro_count, top_count, row_count, capacity, place_ref, *refs):
    count = (len(refs) - 6) // 3
    rows_refs, ids_refs, (router_ref, gate_ref, up_ref, down_ref), out_refs = (
        refs[:count], refs[count : 2 * count], refs[2 * count : 2 * count + 4], refs[2 * count + 4 : -2]
    )
    rows_ref, hidden_ref = refs[-2:]
    inner_width, width = down_ref.shape
    inner_step, outer_step = 512, 512
    total_rows = rows_ref.shape[0]
    part_rows = total_rows // count
    expert_count = router_ref.shape[0]
    for i, ref in enumerate(rows_refs):
        rows_ref[i * part_rows : (i + 1) * part_rows, :] = ref[:, :width]

    owner, micro = owner_of(place_ref), micro_at(moment, micro_count, place_ref)
    ids = jnp.concatenate([ref[:, ref.shape[1] - lanes :].astype(jnp.float32) for ref in ids_refs], axis=0)
    names = lax.broadcasted_iota(jnp.int32, (total_rows, expert_count), 1).astype(jnp.float32)
    member = jnp.zeros((total_rows, expert_count), jnp.float32)
    for k in range(top_count):
        choice = ids[:, k : k + 1]
        for m in range(1, micro_count):
            at = m * top_count + k
            choice = jnp.where(micro == m, ids[:, at : at + 1], choice)
        member = jnp.where(choice == names, 1.0, member)
    mine = names == owner.astype(jnp.float32)
    row_at = lax.broadcasted_iota(jnp.int32, (total_rows, total_rows), 0)
    column_at = lax.broadcasted_iota(jnp.int32, (total_rows, total_rows), 1)
    before = (column_at < row_at) & (column_at // row_count == row_at // row_count)
    named = jnp.where(mine, member, 0.0)
    earlier = jnp.dot(
        jnp.where(before, 1.0, 0.0).astype(jnp.bfloat16), named.astype(jnp.bfloat16), preferred_element_type=jnp.float32
    )
    slot = jnp.sum(jnp.where(mine, earlier, 0.0), axis=1, keepdims=True)
    kept = (jnp.sum(named, axis=1, keepdims=True) > 0.5) & (slot < capacity - 0.5)
    logits = lax.dot_general(rows_ref[...], router_ref[...], (((1,), (1,)), ((), ())), preferred_element_type=jnp.float32)
    scores = jax.nn.sigmoid(logits)
    total = jnp.sum(jnp.where(member > 0.5, scores, 0.0), axis=1, keepdims=True)
    own = jnp.sum(jnp.where(mine, scores, 0.0), axis=1, keepdims=True)
    factor = jnp.where(kept, routed_scale * own / total, 0.0)

    for at in range(0, inner_width, inner_step):
        part = slice(at, at + inner_step)
        gate_part = jnp.dot(rows_ref[...], gate_ref[:, part], preferred_element_type=jnp.float32)
        up_part = jnp.dot(rows_ref[...], up_ref[:, part], preferred_element_type=jnp.float32)
        hidden = gate_part / (1.0 + jnp.exp(-gate_part)) * up_part
        hidden_ref[:, part] = jnp.where(kept, hidden * factor, 0.0).astype(jnp.bfloat16)
    hidden = hidden_ref[...]
    for at in range(0, width, outer_step):
        part = slice(at, at + outer_step)
        share = jnp.dot(hidden, down_ref[:, part], preferred_element_type=jnp.float32)
        for i, out_ref in enumerate(out_refs):
            out_ref[:, part] = share[i * part_rows : (i + 1) * part_rows].astype(out_ref.dtype)


def expert_shares(moment, micro_count, top_count, row_count, capacity, place, rows, ids, weights):
    part_rows = rows[0].shape[0]
    inner_width, width = weights[3].shape
    total_rows = len(rows) * part_rows
    return pl.pallas_call(
        functools.partial(expert_kernel, moment, micro_count, top_count, row_count, capacity),
        out_shape=[
            jax.ShapeDtypeStruct((part_rows, width), jnp.bfloat16 if i % cores else jnp.float32) for i in range(len(rows))
        ],
        in_specs=[in_vmem] * (1 + 2 * len(rows) + 4),
        out_specs=[in_vmem] * len(rows),
        scratch_shapes=[pltpu.VMEM((total_rows, width), jnp.bfloat16), pltpu.VMEM((total_rows, inner_width), jnp.bfloat16)],
        compiler_params=pltpu.CompilerParams(vmem_limit_bytes=10 * 1024 * 1024),
        cost_estimate=pl.CostEstimate(
            flops=6 * total_rows * width * inner_width, bytes_accessed=6 * width * inner_width, transcendentals=0
        ),
    )(place, *rows, *ids, *weights)


def chip_kernel(own_ref, other_ref, out_ref):
    out_ref[...] = (own_ref[...] + other_ref[...].astype(jnp.float32)).astype(jnp.bfloat16)


def chip_shares(own, other):
    return pl.pallas_call(
        chip_kernel,
        out_shape=jax.ShapeDtypeStruct(other.shape, jnp.bfloat16),
        in_specs=[in_vmem] * 2,
        out_specs=in_vmem,
        compiler_params=pltpu.CompilerParams(vmem_limit_bytes=6 * 1024 * 1024),
    )(own, other)


def spread_kernel(inner, entering, place_ref, hidden_ref, *refs):
    out_refs = refs[-outer_size:]
    refs = refs[:-outer_size]
    if entering is not None:
        *refs, tokens_ref = refs
    total = refs[0][...]
    for ref in refs[1:]:
        total = total + ref[...].astype(jnp.float32)
    row_count = hidden_ref.shape[0]
    blocks = [total[o * row_count : (o + 1) * row_count] for o in range(outer_size)]
    here = outer_is(place_ref, inner)
    for k, out_ref in enumerate(out_refs):
        block = blocks[k]
        for o in range(1, outer_size):
            block = jnp.where(here[o], blocks[(o + k) % outer_size], block)
        if k == 0:
            block = block + hidden_ref[...].astype(jnp.float32)
            if entering is not None:
                block = jnp.where(section_of(place_ref) == entering, tokens_ref[...].astype(jnp.float32), block)
        out_ref[...] = block.astype(out_ref.dtype)


def spread(inner, entering, stays, place, hidden, shares, *tokens):
    return pl.pallas_call(
        functools.partial(spread_kernel, inner, entering),
        out_shape=[
            jax.ShapeDtypeStruct(hidden.shape, jnp.float32 if stays and k == 0 else jnp.bfloat16) for k in range(outer_size)
        ],
        in_specs=[in_vmem] * (2 + len(shares) + len(tokens)),
        out_specs=[in_vmem] * outer_size,
        compiler_params=pltpu.CompilerParams(vmem_limit_bytes=8 * 1024 * 1024),
    )(place, hidden, *shares, *tokens)


def landed(refs):
    total = refs[0][...].astype(jnp.float32)
    for ref in refs[1:]:
        total = total + ref[...].astype(jnp.float32)
    return total.astype(jnp.bfloat16)


def land_kernel(place_ref, gain_ref, *refs):
    *refs, hidden_ref, out_ref = refs
    hidden = landed(refs[:outer_size])
    if len(refs) > outer_size:
        hidden = jnp.where(section_of(place_ref) == 0, refs[outer_size][...], hidden)
    hidden_ref[...] = hidden
    out_ref[...] = normalize(hidden.astype(jnp.float32), gain_ref[...].astype(jnp.float32)).astype(jnp.bfloat16)


def land(place, gain, parts, *waiting):
    return pl.pallas_call(
        land_kernel,
        out_shape=[jax.ShapeDtypeStruct(parts[0].shape, jnp.bfloat16)] * 2,
        in_specs=[in_vmem] * (2 + len(parts) + len(waiting)),
        out_specs=[in_vmem] * 2,
        compiler_params=pltpu.CompilerParams(vmem_limit_bytes=4 * 1024 * 1024),
    )(place, gain, *parts, *waiting)


def finish_kernel(final, place_ref, *refs):
    *refs, out_ref = refs
    result = landed(refs[:outer_size])
    if len(refs) > outer_size:
        result = jnp.where(section_of(place_ref) == final, result, refs[outer_size][...])
    out_ref[...] = result


def finish(final, place, parts, *mixed):
    return pl.pallas_call(
        functools.partial(finish_kernel, final),
        out_shape=jax.ShapeDtypeStruct(parts[0].shape, jnp.bfloat16),
        in_specs=[in_vmem] * (1 + len(parts) + len(mixed)),
        out_specs=in_vmem,
        compiler_params=pltpu.CompilerParams(vmem_limit_bytes=4 * 1024 * 1024),
    )(place, *parts, *mixed)


def per_device(tokens, norm_gain, router, w_gate, w_up, w_down, expert_ids):
    sections = lax.axis_size("section")
    section_index = lax.axis_index("section")
    expert_count = lax.axis_size("expert")
    owner = lax.axis_index("expert")
    micro_count = expert_ids.shape[1]
    row_count = tokens.shape[1]
    width = tokens.shape[2]
    top_count = expert_ids.shape[3]
    capacity = min(row_count, max(2, 5 * row_count * top_count // (4 * expert_count)))
    router_rows = jnp.transpose(router[0])
    gate, up, down = (w[0, 0] for w in (w_gate, w_up, w_down))
    own_ids = expert_ids[0]
    inner = expert_count // outer_size
    swap = [(e, e + 1 - 2 * (e % cores)) for e in range(expert_count)]

    def swapped(rows):
        return lax.ppermute(rows, "expert", swap)

    def along_x(rows, shift):
        pairs = [(e, e // inner * inner + (e + shift * cores) % inner) for e in range(expert_count)]
        return lax.ppermute(rows, "expert", pairs)

    def sent(rows, route, shift):
        pairs = [
            (a * expert_count + e, b * expert_count + (e + shift * inner) % expert_count)
            for a, b in route
            for e in range(expert_count)
        ]
        return lax.ppermute(rows, ("section", "expert"), pairs)

    place = jnp.where(jnp.arange(lanes, dtype=jnp.int32)[None] == 0, owner, section_index).astype(jnp.int32)
    stay = [(s, s) for s in range(sections)]
    incoming = tokens[0]
    mixed = ids = None
    final = sections - 1
    places = inner // cores
    total_moments = sections + micro_count - 1
    for moment in range(total_moments):
        if moment == 0:
            normed, place = first_norm(place, incoming, norm_gain, own_ids)
        blocks = [normed] + [sent(normed, stay, k) for k in range(1, outer_size)]
        if moment == 0:
            place, (router_held, gate_held) = hold(place, (router_rows, gate))
        ordered = in_order(inner, place, blocks)
        if moment == 0:
            ordered, place = lax.optimization_barrier((ordered, place))
        rows = [ordered, swapped(ordered)]
        coming = [along_x(ordered, h) for h in range(1, places)]
        if moment == 0:
            place, (up_held, down_held) = hold(place, (up, down))
            weights = (router_held, gate_held, up_held, down_held)
            coming, place = lax.optimization_barrier((coming, place))
        rows += [r for row in coming for r in (row, swapped(row))]
        ids = rows if ids is None else ids
        shares = expert_shares(moment, micro_count, top_count, row_count, capacity, place, rows, ids, weights)

        away = [chip_shares(shares[h * cores], swapped(shares[h * cores + 1])) for h in range(1, places)]
        arrived = [along_x(share, -h) for h, share in enumerate(away, 1)]
        shares = [shares[0], swapped(shares[1]), *arrived]
        entering, finished = moment + 1, moment - final
        last = finished == micro_count - 1
        joint = sections == 2 and entering == final
        parts = spread(inner, final if joint else None, last, place, incoming, shares, *([tokens[0]] if joint else []))
        if last:
            parts = [sent(part, stay, k) if k else part for k, part in enumerate(parts)]
            mixed = finish(final, place, parts, *([] if mixed is None else [mixed]))
            break
        route = [(s, s + 1) for s in range(sections - 1)]
        back = [(final, 0)]
        waiting = []
        if not joint and entering < micro_count:
            waiting = [sent(tokens[0], [(entering, 0)], 0)]
        if finished > 0:
            result = sum(sent(part, [(final, finished)], k).astype(jnp.float32) for k, part in enumerate(parts))
            mixed = jnp.where(section_index == finished, result.astype(jnp.bfloat16), mixed)
        parts = [
            sent(part, route + back if finished == 0 or (joint and k == 0) else route, k) for k, part in enumerate(parts)
        ]
        incoming, normed = land(place, norm_gain, parts, *waiting)
        if finished == 0:
            mixed = incoming
    return mixed[None]


def solution(mesh):
    placed = (
        P("section", "expert", None),
        P("section", None),
        P("section", None, None),
        P("section", "expert", None, None),
        P("section", "expert", None, None),
        P("section", "expert", None, None),
        P("section", None, "expert", None),
    )
    return jax.shard_map(
        per_device,
        mesh=mesh,
        in_specs=placed,
        out_specs=P("section", "expert", None),
        check_vma=False,
    )
```

```python
import functools

import jax
import jax.numpy as jnp
from jax import lax
from jax.experimental import pallas as pl
from jax.experimental.pallas import tpu as pltpu
from jax.sharding import PartitionSpec as P

epsilon = 1e-06
routed_scale = 2.5
lanes = 128
outer_size = 4
cores = 2
in_vmem = pl.BlockSpec(memory_space=pltpu.VMEM)
in_hbm = pl.BlockSpec(memory_space=pltpu.HBM)


def hbm(array):
    return pltpu.with_memory_space_constraint(array, pltpu.HBM)


def owner_of(place_ref):
    return place_ref[0:1, 0:1]


def section_of(place_ref):
    return place_ref[0:1, 1:2]


def micro_at(moment, micro_count, place_ref):
    return jnp.minimum(jnp.maximum(moment - section_of(place_ref), 0), micro_count - 1)


def normalize(values, gain):
    inverse_rms = lax.rsqrt(jnp.mean(values * values, axis=-1, keepdims=True) + epsilon)
    return values * inverse_rms * gain


def start_all(copies):
    for copy in copies:
        copy.start()


def wait_all(copies):
    for copy in copies:
        copy.wait()


def core_of(place_ref):
    return lax.rem(owner_of(place_ref), cores)


def paired(place_ref, own, other):
    first = core_of(place_ref) == 0
    return jnp.concatenate([jnp.where(first, own, other), jnp.where(first, other, own)], axis=0)


def first_norm_kernel(place_ref, gain_ref, tokens_ref, other_tokens_ref, ids_ref, other_ids_ref, hidden_ref, out_ref, place_out):
    place_out[...] = place_ref[...]
    width = tokens_ref.shape[1]
    hidden = paired(place_ref, tokens_ref[...].astype(jnp.float32), other_tokens_ref[...].astype(jnp.float32))
    hidden_ref[...] = hidden.astype(jnp.bfloat16)
    out_ref[:, :width] = normalize(hidden, gain_ref[...].astype(jnp.float32)).astype(jnp.bfloat16)
    micro_count, _, top_count = ids_ref.shape
    lane_at = lax.broadcasted_iota(jnp.int32, (hidden.shape[0], lanes), 1)
    named = jnp.zeros((hidden.shape[0], lanes), jnp.float32)
    for m in range(micro_count):
        choices = paired(place_ref, ids_ref[m].astype(jnp.float32), other_ids_ref[m].astype(jnp.float32))
        for k in range(top_count):
            named = jnp.where(lane_at == m * top_count + k, choices[:, k : k + 1], named)
    out_ref[:, width:] = named.astype(jnp.bfloat16)


def first_norm(place, gain, tokens, other_tokens, ids, other_ids):
    row_count, width = tokens.shape
    return pl.pallas_call(
        first_norm_kernel,
        out_shape=[
            jax.ShapeDtypeStruct((cores * row_count, width), jnp.bfloat16),
            jax.ShapeDtypeStruct((cores * row_count, width + lanes), jnp.bfloat16),
            jax.ShapeDtypeStruct(place.shape, place.dtype),
        ],
        in_specs=[in_vmem] * 6,
        out_specs=[in_vmem] * 3,
        compiler_params=pltpu.CompilerParams(vmem_limit_bytes=4 * 1024 * 1024),
    )(place, gain, tokens, other_tokens, ids, other_ids)


def hold_kernel(place_ref, *refs):
    count = (len(refs) - 2) // 2
    sources, place_out, targets, sems = refs[:count], refs[count], refs[count + 1 : -1], refs[-1]
    copies = [pltpu.make_async_copy(source, target, sems.at[i]) for i, (source, target) in enumerate(zip(sources, targets))]
    start_all(copies)
    place_out[...] = place_ref[...]
    wait_all(copies)


def hold(place, arrays):
    place, *held = pl.pallas_call(
        hold_kernel,
        out_shape=[jax.ShapeDtypeStruct(x.shape, x.dtype) for x in (place, *arrays)],
        in_specs=[in_vmem] + [in_hbm] * len(arrays),
        out_specs=[in_vmem] * (1 + len(arrays)),
        scratch_shapes=[pltpu.SemaphoreType.DMA((len(arrays),))],
        compiler_params=pltpu.CompilerParams(vmem_limit_bytes=1024 * 1024),
        cost_estimate=pl.CostEstimate(
            flops=0, bytes_accessed=2 * sum(x.size * x.dtype.itemsize for x in arrays), transcendentals=0
        ),
    )(place, *[hbm(x) for x in arrays])
    return place, held


def expert_kernel(moment, micro_count, top_count, row_count, capacity, place_ref, *refs):
    *refs, router_ref, gate_ref, up_ref, down_ref, own_ref, other_ref, rows_ref, hidden_ref = refs
    count = len(refs) // 2
    rows_refs, ids_refs = refs[:count], refs[count:]
    inner_width, width = down_ref.shape
    inner_step, outer_step = 512, 512
    total_rows = rows_ref.shape[0]
    part_rows = total_rows // count
    expert_count = router_ref.shape[0]
    for i, ref in enumerate(rows_refs):
        rows_ref[i * part_rows : (i + 1) * part_rows, :] = ref[:, :width]

    owner, micro = owner_of(place_ref), micro_at(moment, micro_count, place_ref)
    ids = jnp.concatenate([ref[:, ref.shape[1] - lanes :].astype(jnp.float32) for ref in ids_refs], axis=0)
    names = lax.broadcasted_iota(jnp.int32, (total_rows, expert_count), 1).astype(jnp.float32)
    member = jnp.zeros((total_rows, expert_count), jnp.float32)
    for k in range(top_count):
        choice = ids[:, k : k + 1]
        for m in range(1, micro_count):
            at = m * top_count + k
            choice = jnp.where(micro == m, ids[:, at : at + 1], choice)
        member = jnp.where(choice == names, 1.0, member)
    mine = names == owner.astype(jnp.float32)
    row_at = lax.broadcasted_iota(jnp.int32, (total_rows, total_rows), 0)
    column_at = lax.broadcasted_iota(jnp.int32, (total_rows, total_rows), 1)
    before = (column_at < row_at) & (column_at // row_count == row_at // row_count)
    named = jnp.where(mine, member, 0.0)
    earlier = jnp.dot(
        jnp.where(before, 1.0, 0.0).astype(jnp.bfloat16), named.astype(jnp.bfloat16), preferred_element_type=jnp.float32
    )
    slot = jnp.sum(jnp.where(mine, earlier, 0.0), axis=1, keepdims=True)
    kept = (jnp.sum(named, axis=1, keepdims=True) > 0.5) & (slot < capacity - 0.5)
    logits = lax.dot_general(rows_ref[...], router_ref[...], (((1,), (1,)), ((), ())), preferred_element_type=jnp.float32)
    scores = jax.nn.sigmoid(logits)
    total = jnp.sum(jnp.where(member > 0.5, scores, 0.0), axis=1, keepdims=True)
    own = jnp.sum(jnp.where(mine, scores, 0.0), axis=1, keepdims=True)
    factor = jnp.where(kept, routed_scale * own / total, 0.0)

    for at in range(0, inner_width, inner_step):
        part = slice(at, at + inner_step)
        gate_part = jnp.dot(rows_ref[...], gate_ref[:, part], preferred_element_type=jnp.float32)
        up_part = jnp.dot(rows_ref[...], up_ref[:, part], preferred_element_type=jnp.float32)
        hidden = gate_part / (1.0 + jnp.exp(-gate_part)) * up_part
        hidden_ref[:, part] = jnp.where(kept, hidden * factor, 0.0).astype(jnp.bfloat16)
    hidden = hidden_ref[...]
    for at in range(0, width, outer_step):
        part = slice(at, at + outer_step)
        share = jnp.dot(hidden, down_ref[:, part], preferred_element_type=jnp.float32)
        own_ref[:, part] = share[: total_rows // cores]
        other_ref[:, part] = share[total_rows // cores :].astype(jnp.bfloat16)


def expert_shares(moment, micro_count, top_count, row_count, capacity, place, rows, ids, weights):
    part_rows = rows[0].shape[0]
    inner_width, width = weights[3].shape
    total_rows = len(rows) * part_rows
    return pl.pallas_call(
        functools.partial(expert_kernel, moment, micro_count, top_count, row_count, capacity),
        out_shape=[jax.ShapeDtypeStruct((total_rows // cores, width), kind) for kind in (jnp.float32, jnp.bfloat16)],
        in_specs=[in_vmem] * (1 + 2 * len(rows) + 4),
        out_specs=[in_vmem] * 2,
        scratch_shapes=[pltpu.VMEM((total_rows, width), jnp.bfloat16), pltpu.VMEM((total_rows, inner_width), jnp.bfloat16)],
        compiler_params=pltpu.CompilerParams(vmem_limit_bytes=10 * 1024 * 1024),
        cost_estimate=pl.CostEstimate(
            flops=6 * total_rows * width * inner_width, bytes_accessed=6 * width * inner_width, transcendentals=0
        ),
    )(place, *rows, *ids, *weights)


def spread_kernel(entering, place_ref, hidden_ref, own_ref, other_ref, *refs):
    rows = hidden_ref.shape[0]
    if entering is not None:
        tokens_ref, *refs = refs
    for i, out_ref in enumerate(refs):
        part = slice(i * rows, (i + 1) * rows)
        block = own_ref[part, :] + other_ref[part, :].astype(jnp.float32)
        if i == 0:
            block = jnp.where(core_of(place_ref) == 0, block + hidden_ref[...].astype(jnp.float32), block)
            if entering is not None:
                block = jnp.where(section_of(place_ref) == entering, tokens_ref[...].astype(jnp.float32), block)
        out_ref[...] = block.astype(jnp.bfloat16)


def spread(entering, place, hidden, own, other, *tokens):
    count = own.shape[0] // hidden.shape[0]
    return pl.pallas_call(
        functools.partial(spread_kernel, entering),
        out_shape=[jax.ShapeDtypeStruct(hidden.shape, jnp.bfloat16)] * count,
        in_specs=[in_vmem] * (4 + len(tokens)),
        out_specs=[in_vmem] * count,
        compiler_params=pltpu.CompilerParams(vmem_limit_bytes=8 * 1024 * 1024),
    )(place, hidden, own, other, *tokens)


def partial_kernel(*refs):
    *refs, out_ref = refs
    total = refs[0][...].astype(jnp.float32)
    for ref in refs[1:]:
        total = total + ref[...].astype(jnp.float32)
    out_ref[...] = total.astype(jnp.bfloat16)


def partial_sum(parts):
    return pl.pallas_call(
        partial_kernel,
        out_shape=jax.ShapeDtypeStruct(parts[0].shape, jnp.bfloat16),
        in_specs=[in_vmem] * len(parts),
        out_specs=in_vmem,
        compiler_params=pltpu.CompilerParams(vmem_limit_bytes=4 * 1024 * 1024),
    )(*parts)


def both(one_ref, two_ref):
    return one_ref[...].astype(jnp.float32) + two_ref[...].astype(jnp.float32)


def land_kernel(place_ref, gain_ref, one_ref, two_ref, *refs):
    *waiting, hidden_ref, out_ref = refs
    hidden = both(one_ref, two_ref)
    if waiting:
        hidden = jnp.where(section_of(place_ref) == 0, waiting[0][...].astype(jnp.float32), hidden)
    hidden_ref[...] = hidden.astype(jnp.bfloat16)
    hidden = hidden.astype(jnp.bfloat16).astype(jnp.float32)
    out_ref[...] = normalize(hidden, gain_ref[...].astype(jnp.float32)).astype(jnp.bfloat16)


def land(place, gain, one, two, *waiting):
    return pl.pallas_call(
        land_kernel,
        out_shape=[jax.ShapeDtypeStruct(one.shape, jnp.bfloat16)] * 2,
        in_specs=[in_vmem] * (4 + len(waiting)),
        out_specs=[in_vmem] * 2,
        compiler_params=pltpu.CompilerParams(vmem_limit_bytes=4 * 1024 * 1024),
    )(place, gain, one, two, *waiting)


def finish_kernel(final, place_ref, one_ref, two_ref, *refs):
    *mixed, out_ref = refs
    row_count = out_ref.shape[0]
    result = both(one_ref, two_ref).astype(jnp.bfloat16).astype(jnp.float32)
    if mixed:
        result = jnp.where(section_of(place_ref) == final, result, mixed[0][...].astype(jnp.float32))
    result = jnp.where(core_of(place_ref) == 0, result[:row_count], result[row_count:])
    out_ref[...] = result.astype(jnp.bfloat16)


def finish(final, place, one, two, *mixed):
    rows, width = one.shape
    return pl.pallas_call(
        functools.partial(finish_kernel, final),
        out_shape=jax.ShapeDtypeStruct((rows // cores, width), jnp.bfloat16),
        in_specs=[in_vmem] * (3 + len(mixed)),
        out_specs=in_vmem,
        compiler_params=pltpu.CompilerParams(vmem_limit_bytes=4 * 1024 * 1024),
    )(place, one, two, *mixed)


def per_device(tokens, norm_gain, router, w_gate, w_up, w_down, expert_ids):
    sections = lax.axis_size("section")
    section_index = lax.axis_index("section")
    expert_count = lax.axis_size("expert")
    owner = lax.axis_index("expert")
    micro_count = expert_ids.shape[1]
    row_count = tokens.shape[1]
    width = tokens.shape[2]
    top_count = expert_ids.shape[3]
    capacity = min(row_count, max(2, 5 * row_count * top_count // (4 * expert_count)))
    router_rows = jnp.transpose(router[0])
    gate, up, down = (w[0, 0] for w in (w_gate, w_up, w_down))
    own_ids = expert_ids[0]
    inner = expert_count // outer_size
    swap = [(e, e + 1 - 2 * (e % cores)) for e in range(expert_count)]

    def swapped(rows):
        return lax.ppermute(rows, "expert", swap)

    places = inner // cores
    steps = [(j, k) for j in range(places // cores) for k in range(outer_size)]

    def sent(rows, route, step, sign, first_core=()):
        j, k = step
        pairs = []
        for a, b in (*route, *first_core):
            for e in range(expert_count):
                o, x, c = e // inner, e % inner // cores, e % cores
                o = (o + sign * k) % outer_size
                x = (x + sign * (c * (places // cores) + j)) % places
                if c == 0 or (a, b) in route:
                    pairs.append((a * expert_count + e, b * expert_count + o * inner + x * cores + c))
        return lax.ppermute(rows, ("section", "expert"), pairs)

    place = jnp.where(jnp.arange(lanes, dtype=jnp.int32)[None] == 0, owner, section_index).astype(jnp.int32)
    stay = [(s, s) for s in range(sections)]
    mixed = ids = None
    final = sections - 1
    total_moments = sections + micro_count - 1
    for moment in range(total_moments):
        if moment == 0:
            incoming, normed, place = first_norm(
                place, norm_gain, tokens[0], swapped(tokens[0]), own_ids, swapped(own_ids)
            )
            entering_rows = incoming
        rows = [sent(normed, stay, step, 1) for step in steps]
        if moment == 0:
            place, weights = hold(place, (router_rows, gate, up, down))
            rows, place = lax.optimization_barrier((rows, place))
        rows = list(rows) + [swapped(row) for row in rows]
        ids = rows if ids is None else ids
        own, other = expert_shares(moment, micro_count, top_count, row_count, capacity, place, rows, ids, weights)

        entering, finished = moment + 1, moment - final
        last = finished == micro_count - 1
        joint = sections == 2 and entering == final
        parts = spread(
            final if joint else None, place, incoming, own, swapped(other), *([entering_rows] if joint else [])
        )

        def arrived(route, first_core=(), parts=parts):
            moved = [sent(part, route, step, -1, () if any(step) else first_core) for step, part in zip(steps, parts)]
            part = partial_sum(moved)
            return part, swapped(part)

        if last:
            mixed = finish(final, place, *arrived(stay), *([] if mixed is None else [mixed]))
            break
        route = [(s, s + 1) for s in range(sections - 1)]
        back = [(final, 0)]
        waiting = []
        if not joint and entering < micro_count:
            waiting = [sent(entering_rows, [], steps[0], -1, [(entering, 0)])]
            waiting = [jnp.where(owner % cores == 0, waiting[0], swapped(waiting[0]))]
        if finished > 0:
            one, two = arrived([(final, finished)])
            mixed = jnp.where(section_index == finished, (one.astype(jnp.float32) + two.astype(jnp.float32)).astype(jnp.bfloat16), mixed)
        one, two = arrived(route + back if finished == 0 else route, back if joint else ())
        incoming, normed = land(place, norm_gain, one, two, *waiting)
        if finished == 0:
            mixed = incoming
    return mixed[None]


def solution(mesh):
    placed = (
        P("section", "expert", None),
        P("section", None),
        P("section", None, None),
        P("section", "expert", None, None),
        P("section", "expert", None, None),
        P("section", "expert", None, None),
        P("section", None, "expert", None),
    )
    return jax.shard_map(
        per_device,
        mesh=mesh,
        in_specs=placed,
        out_specs=P("section", "expert", None),
        check_vma=False,
    )
```

```python
import functools

import jax
import jax.numpy as jnp
from jax import lax
from jax.experimental import pallas as pl
from jax.experimental.pallas import tpu as pltpu
from jax.sharding import PartitionSpec as P

epsilon = 1e-06
routed_scale = 2.5
lanes = 128
outer_size = 4
cores = 2
in_vmem = pl.BlockSpec(memory_space=pltpu.VMEM)
in_hbm = pl.BlockSpec(memory_space=pltpu.HBM)


def hbm(array):
    return pltpu.with_memory_space_constraint(array, pltpu.HBM)


def owner_of(place_ref):
    return place_ref[0:1, 0:1]


def section_of(place_ref):
    return place_ref[0:1, 1:2]


def micro_at(moment, micro_count, place_ref):
    return jnp.minimum(jnp.maximum(moment - section_of(place_ref), 0), micro_count - 1)


def normalize(values, gain):
    inverse_rms = lax.rsqrt(jnp.mean(values * values, axis=-1, keepdims=True) + epsilon)
    return values * inverse_rms * gain


def start_all(copies):
    for copy in copies:
        copy.start()


def wait_all(copies):
    for copy in copies:
        copy.wait()


def core_of(place_ref):
    return lax.rem(owner_of(place_ref), cores)


def paired(place_ref, own, other):
    first = core_of(place_ref) == 0
    return jnp.concatenate([jnp.where(first, own, other), jnp.where(first, other, own)], axis=0)


def first_norm_kernel(place_ref, gain_ref, tokens_ref, other_tokens_ref, ids_ref, other_ids_ref, hidden_ref, out_ref, place_out):
    place_out[...] = place_ref[...]
    width = tokens_ref.shape[1]
    hidden = paired(place_ref, tokens_ref[...].astype(jnp.float32), other_tokens_ref[...].astype(jnp.float32))
    hidden_ref[...] = hidden.astype(jnp.bfloat16)
    out_ref[:, :width] = normalize(hidden, gain_ref[...].astype(jnp.float32)).astype(jnp.bfloat16)
    micro_count, _, top_count = ids_ref.shape
    lane_at = lax.broadcasted_iota(jnp.int32, (hidden.shape[0], lanes), 1)
    named = jnp.zeros((hidden.shape[0], lanes), jnp.float32)
    for m in range(micro_count):
        choices = paired(place_ref, ids_ref[m].astype(jnp.float32), other_ids_ref[m].astype(jnp.float32))
        for k in range(top_count):
            named = jnp.where(lane_at == m * top_count + k, choices[:, k : k + 1], named)
    out_ref[:, width:] = named.astype(jnp.bfloat16)


def first_norm(place, gain, tokens, other_tokens, ids, other_ids):
    row_count, width = tokens.shape
    return pl.pallas_call(
        first_norm_kernel,
        out_shape=[
            jax.ShapeDtypeStruct((cores * row_count, width), jnp.bfloat16),
            jax.ShapeDtypeStruct((cores * row_count, width + lanes), jnp.bfloat16),
            jax.ShapeDtypeStruct(place.shape, place.dtype),
        ],
        in_specs=[in_vmem] * 6,
        out_specs=[in_vmem] * 3,
        compiler_params=pltpu.CompilerParams(vmem_limit_bytes=4 * 1024 * 1024),
    )(place, gain, tokens, other_tokens, ids, other_ids)


def hold_kernel(place_ref, *refs):
    count = (len(refs) - 2) // 2
    sources, place_out, targets, sems = refs[:count], refs[count], refs[count + 1 : -1], refs[-1]
    copies = [pltpu.make_async_copy(source, target, sems.at[i]) for i, (source, target) in enumerate(zip(sources, targets))]
    start_all(copies)
    place_out[...] = place_ref[...]
    wait_all(copies)


def hold(place, arrays):
    place, *held = pl.pallas_call(
        hold_kernel,
        out_shape=[jax.ShapeDtypeStruct(x.shape, x.dtype) for x in (place, *arrays)],
        in_specs=[in_vmem] + [in_hbm] * len(arrays),
        out_specs=[in_vmem] * (1 + len(arrays)),
        scratch_shapes=[pltpu.SemaphoreType.DMA((len(arrays),))],
        compiler_params=pltpu.CompilerParams(vmem_limit_bytes=1024 * 1024),
        cost_estimate=pl.CostEstimate(
            flops=0, bytes_accessed=2 * sum(x.size * x.dtype.itemsize for x in arrays), transcendentals=0
        ),
    )(place, *[hbm(x) for x in arrays])
    return place, held


def expert_kernel(moment, micro_count, top_count, row_count, capacity, place_ref, *refs):
    *refs, router_ref, gate_ref, up_ref, down_ref, own_ref, other_ref, rows_ref, hidden_ref = refs
    count = len(refs) // 2
    rows_refs, ids_refs = refs[:count], refs[count:]
    inner_width, width = down_ref.shape
    inner_step, outer_step = 512, 512
    total_rows = rows_ref.shape[0]
    part_rows = total_rows // count
    expert_count = router_ref.shape[0]
    for i, ref in enumerate(rows_refs):
        rows_ref[i * part_rows : (i + 1) * part_rows, :] = ref[:, :width]

    owner, micro = owner_of(place_ref), micro_at(moment, micro_count, place_ref)
    ids = jnp.concatenate([ref[:, ref.shape[1] - lanes :].astype(jnp.float32) for ref in ids_refs], axis=0)
    names = lax.broadcasted_iota(jnp.int32, (total_rows, expert_count), 1).astype(jnp.float32)
    member = jnp.zeros((total_rows, expert_count), jnp.float32)
    for k in range(top_count):
        choice = ids[:, k : k + 1]
        for m in range(1, micro_count):
            at = m * top_count + k
            choice = jnp.where(micro == m, ids[:, at : at + 1], choice)
        member = jnp.where(choice == names, 1.0, member)
    mine = names == owner.astype(jnp.float32)
    row_at = lax.broadcasted_iota(jnp.int32, (total_rows, total_rows), 0)
    column_at = lax.broadcasted_iota(jnp.int32, (total_rows, total_rows), 1)
    before = (column_at < row_at) & (column_at // row_count == row_at // row_count)
    named = jnp.where(mine, member, 0.0)
    earlier = jnp.dot(
        jnp.where(before, 1.0, 0.0).astype(jnp.bfloat16), named.astype(jnp.bfloat16), preferred_element_type=jnp.float32
    )
    slot = jnp.sum(jnp.where(mine, earlier, 0.0), axis=1, keepdims=True)
    kept = (jnp.sum(named, axis=1, keepdims=True) > 0.5) & (slot < capacity - 0.5)
    logits = lax.dot_general(rows_ref[...], router_ref[...], (((1,), (1,)), ((), ())), preferred_element_type=jnp.float32)
    scores = jax.nn.sigmoid(logits)
    total = jnp.sum(jnp.where(member > 0.5, scores, 0.0), axis=1, keepdims=True)
    own = jnp.sum(jnp.where(mine, scores, 0.0), axis=1, keepdims=True)
    factor = jnp.where(kept, routed_scale * own / total, 0.0)

    for at in range(0, inner_width, inner_step):
        part = slice(at, at + inner_step)
        gate_part = jnp.dot(rows_ref[...], gate_ref[:, part], preferred_element_type=jnp.float32)
        up_part = jnp.dot(rows_ref[...], up_ref[:, part], preferred_element_type=jnp.float32)
        hidden = gate_part / (1.0 + jnp.exp(-gate_part)) * up_part
        hidden_ref[:, part] = jnp.where(kept, hidden * factor, 0.0).astype(jnp.bfloat16)
    hidden = hidden_ref[...]
    for at in range(0, width, outer_step):
        part = slice(at, at + outer_step)
        share = jnp.dot(hidden, down_ref[:, part], preferred_element_type=jnp.float32)
        own_ref[:, part] = share[: total_rows // cores]
        other_ref[:, part] = share[total_rows // cores :].astype(jnp.bfloat16)


def expert_shares(moment, micro_count, top_count, row_count, capacity, place, rows, ids, weights):
    part_rows = rows[0].shape[0]
    inner_width, width = weights[3].shape
    total_rows = len(rows) * part_rows
    return pl.pallas_call(
        functools.partial(expert_kernel, moment, micro_count, top_count, row_count, capacity),
        out_shape=[jax.ShapeDtypeStruct((total_rows // cores, width), kind) for kind in (jnp.float32, jnp.bfloat16)],
        in_specs=[in_vmem] * (1 + 2 * len(rows) + 4),
        out_specs=[in_vmem] * 2,
        scratch_shapes=[pltpu.VMEM((total_rows, width), jnp.bfloat16), pltpu.VMEM((total_rows, inner_width), jnp.bfloat16)],
        compiler_params=pltpu.CompilerParams(vmem_limit_bytes=10 * 1024 * 1024),
        cost_estimate=pl.CostEstimate(
            flops=6 * total_rows * width * inner_width, bytes_accessed=6 * width * inner_width, transcendentals=0
        ),
    )(place, *rows, *ids, *weights)


def spread_kernel(entering, place_ref, hidden_ref, own_ref, other_ref, *refs):
    rows = hidden_ref.shape[0]
    if entering is not None:
        tokens_ref, *refs = refs
    for i, out_ref in enumerate(refs[::-1]):
        part = slice(i * rows, (i + 1) * rows)
        block = own_ref[part, :] + other_ref[part, :].astype(jnp.float32)
        if i == 0:
            block = jnp.where(core_of(place_ref) == 0, block + hidden_ref[...].astype(jnp.float32), block)
            if entering is not None:
                block = jnp.where(section_of(place_ref) == entering, tokens_ref[...].astype(jnp.float32), block)
        out_ref[...] = block.astype(jnp.bfloat16)


def spread(entering, place, hidden, own, other, *tokens):
    count = own.shape[0] // hidden.shape[0]
    return pl.pallas_call(
        functools.partial(spread_kernel, entering),
        out_shape=[jax.ShapeDtypeStruct(hidden.shape, jnp.bfloat16)] * count,
        in_specs=[in_vmem] * (4 + len(tokens)),
        out_specs=[in_vmem] * count,
        compiler_params=pltpu.CompilerParams(vmem_limit_bytes=8 * 1024 * 1024),
    )(place, hidden, own, other, *tokens)


def partial_kernel(*refs):
    *refs, out_ref = refs
    total = refs[0][...].astype(jnp.float32)
    for ref in refs[1:]:
        total = total + ref[...].astype(jnp.float32)
    out_ref[...] = total.astype(jnp.bfloat16)


def partial_sum(parts):
    return pl.pallas_call(
        partial_kernel,
        out_shape=jax.ShapeDtypeStruct(parts[0].shape, jnp.bfloat16),
        in_specs=[in_vmem] * len(parts),
        out_specs=in_vmem,
        compiler_params=pltpu.CompilerParams(vmem_limit_bytes=4 * 1024 * 1024),
    )(*parts)


def both(one_ref, two_ref):
    return one_ref[...].astype(jnp.float32) + two_ref[...].astype(jnp.float32)


def land_kernel(place_ref, gain_ref, one_ref, two_ref, *refs):
    *waiting, hidden_ref, out_ref = refs
    hidden = both(one_ref, two_ref)
    if waiting:
        hidden = jnp.where(section_of(place_ref) == 0, waiting[0][...].astype(jnp.float32), hidden)
    hidden_ref[...] = hidden.astype(jnp.bfloat16)
    hidden = hidden.astype(jnp.bfloat16).astype(jnp.float32)
    out_ref[...] = normalize(hidden, gain_ref[...].astype(jnp.float32)).astype(jnp.bfloat16)


def land(place, gain, one, two, *waiting):
    return pl.pallas_call(
        land_kernel,
        out_shape=[jax.ShapeDtypeStruct(one.shape, jnp.bfloat16)] * 2,
        in_specs=[in_vmem] * (4 + len(waiting)),
        out_specs=[in_vmem] * 2,
        compiler_params=pltpu.CompilerParams(vmem_limit_bytes=4 * 1024 * 1024),
    )(place, gain, one, two, *waiting)


def finish_kernel(final, place_ref, one_ref, two_ref, *refs):
    *mixed, out_ref = refs
    row_count = out_ref.shape[0]
    result = both(one_ref, two_ref).astype(jnp.bfloat16).astype(jnp.float32)
    if mixed:
        result = jnp.where(section_of(place_ref) == final, result, mixed[0][...].astype(jnp.float32))
    result = jnp.where(core_of(place_ref) == 0, result[:row_count], result[row_count:])
    out_ref[...] = result.astype(jnp.bfloat16)


def finish(final, place, one, two, *mixed):
    rows, width = one.shape
    return pl.pallas_call(
        functools.partial(finish_kernel, final),
        out_shape=jax.ShapeDtypeStruct((rows // cores, width), jnp.bfloat16),
        in_specs=[in_vmem] * (3 + len(mixed)),
        out_specs=in_vmem,
        compiler_params=pltpu.CompilerParams(vmem_limit_bytes=4 * 1024 * 1024),
    )(place, one, two, *mixed)


def per_device(tokens, norm_gain, router, w_gate, w_up, w_down, expert_ids):
    sections = lax.axis_size("section")
    section_index = lax.axis_index("section")
    expert_count = lax.axis_size("expert")
    owner = lax.axis_index("expert")
    micro_count = expert_ids.shape[1]
    row_count = tokens.shape[1]
    width = tokens.shape[2]
    top_count = expert_ids.shape[3]
    capacity = min(row_count, max(2, 5 * row_count * top_count // (4 * expert_count)))
    router_rows = jnp.transpose(router[0])
    gate, up, down = (w[0, 0] for w in (w_gate, w_up, w_down))
    own_ids = expert_ids[0]
    inner = expert_count // outer_size
    swap = [(e, e + 1 - 2 * (e % cores)) for e in range(expert_count)]

    def swapped(rows):
        return lax.ppermute(rows, "expert", swap)

    places = inner // cores
    shifts = sorted(range(outer_size), key=lambda k: -min(k, outer_size - k))
    steps = [(j, k) for k in shifts for j in reversed(range(places // cores))]

    def sent(rows, route, step, sign, first_core=()):
        j, k = step
        pairs = []
        for a, b in (*route, *first_core):
            for e in range(expert_count):
                o, x, c = e // inner, e % inner // cores, e % cores
                o = (o + sign * k) % outer_size
                x = (x + sign * (c * (places // cores) + j)) % places
                if c == 0 or (a, b) in route:
                    pairs.append((a * expert_count + e, b * expert_count + o * inner + x * cores + c))
        return lax.ppermute(rows, ("section", "expert"), pairs)

    place = jnp.where(jnp.arange(lanes, dtype=jnp.int32)[None] == 0, owner, section_index).astype(jnp.int32)
    stay = [(s, s) for s in range(sections)]
    mixed = ids = None
    final = sections - 1
    total_moments = sections + micro_count - 1
    for moment in range(total_moments):
        if moment == 0:
            place, (own_tokens, gain, held_ids) = hold(place, (tokens[0], norm_gain, own_ids))
            incoming, normed, place = first_norm(
                place, gain, own_tokens, swapped(tokens[0]), held_ids, swapped(own_ids)
            )
            entering_rows = incoming
        rows = [sent(normed, stay, step, 1) for step in steps[::-1]]
        if moment == 0:
            place, weights = hold(place, (router_rows, gate, up, down))
            rows, place = lax.optimization_barrier((rows, place))
        rows = list(rows) + [swapped(row) for row in rows]
        ids = rows if ids is None else ids
        own, other = expert_shares(moment, micro_count, top_count, row_count, capacity, place, rows, ids, weights)

        entering, finished = moment + 1, moment - final
        last = finished == micro_count - 1
        joint = sections == 2 and entering == final
        parts = spread(
            final if joint else None, place, incoming, own, swapped(other), *([entering_rows] if joint else [])
        )

        def arrived(route, first_core=(), parts=parts):
            moved = [sent(part, route, step, -1, () if any(step) else first_core) for step, part in zip(steps, parts)]
            part = partial_sum(moved)
            return part, swapped(part)

        if last:
            mixed = finish(final, place, *arrived(stay), *([] if mixed is None else [mixed]))
            break
        route = [(s, s + 1) for s in range(sections - 1)]
        back = [(final, 0)]
        waiting = []
        if not joint and entering < micro_count:
            waiting = [sent(entering_rows, [], steps[-1], -1, [(entering, 0)])]
            waiting = [jnp.where(owner % cores == 0, waiting[0], swapped(waiting[0]))]
        if finished > 0:
            one, two = arrived([(final, finished)])
            mixed = jnp.where(section_index == finished, (one.astype(jnp.float32) + two.astype(jnp.float32)).astype(jnp.bfloat16), mixed)
        one, two = arrived(route + back if finished == 0 else route, back if joint else ())
        incoming, normed = land(place, gain, one, two, *waiting)
        if finished == 0:
            mixed = incoming
    return mixed[None]


def solution(mesh):
    placed = (
        P("section", "expert", None),
        P("section", None),
        P("section", None, None),
        P("section", "expert", None, None),
        P("section", "expert", None, None),
        P("section", "expert", None, None),
        P("section", None, "expert", None),
    )
    return jax.shard_map(
        per_device,
        mesh=mesh,
        in_specs=placed,
        out_specs=P("section", "expert", None),
        check_vma=False,
    )
```

```python
import functools

import jax
import jax.numpy as jnp
from jax import lax
from jax.experimental import pallas as pl
from jax.experimental.pallas import tpu as pltpu
from jax.sharding import PartitionSpec as P

epsilon = 1e-06
routed_scale = 2.5
lanes = 128
outer_size = 4
cores = 2
in_vmem = pl.BlockSpec(memory_space=pltpu.VMEM)
in_hbm = pl.BlockSpec(memory_space=pltpu.HBM)


def hbm(array):
    return pltpu.with_memory_space_constraint(array, pltpu.HBM)


def owner_of(place_ref):
    return place_ref[0:1, 0:1]


def section_of(place_ref):
    return place_ref[0:1, 1:2]


def micro_at(moment, micro_count, place_ref):
    return jnp.minimum(jnp.maximum(moment - section_of(place_ref), 0), micro_count - 1)


def normalize(values, gain):
    inverse_rms = lax.rsqrt(jnp.mean(values * values, axis=-1, keepdims=True) + epsilon)
    return values * inverse_rms * gain


def start_all(copies):
    for copy in copies:
        copy.start()


def wait_all(copies):
    for copy in copies:
        copy.wait()


def core_of(place_ref):
    return lax.rem(owner_of(place_ref), cores)


def paired(place_ref, own, other):
    first = core_of(place_ref) == 0
    return jnp.concatenate([jnp.where(first, own, other), jnp.where(first, other, own)], axis=0)


def first_norm_kernel(place_ref, gain_ref, tokens_ref, other_tokens_ref, ids_ref, other_ids_ref, hidden_ref, out_ref, place_out):
    place_out[...] = place_ref[...]
    width = tokens_ref.shape[1]
    hidden = paired(place_ref, tokens_ref[...].astype(jnp.float32), other_tokens_ref[...].astype(jnp.float32))
    hidden_ref[...] = hidden.astype(jnp.bfloat16)
    out_ref[:, :width] = normalize(hidden, gain_ref[...].astype(jnp.float32)).astype(jnp.bfloat16)
    micro_count, _, top_count = ids_ref.shape
    lane_at = lax.broadcasted_iota(jnp.int32, (hidden.shape[0], lanes), 1)
    named = jnp.zeros((hidden.shape[0], lanes), jnp.float32)
    for m in range(micro_count):
        choices = paired(place_ref, ids_ref[m].astype(jnp.float32), other_ids_ref[m].astype(jnp.float32))
        for k in range(top_count):
            named = jnp.where(lane_at == m * top_count + k, choices[:, k : k + 1], named)
    out_ref[:, width:] = named.astype(jnp.bfloat16)


def first_norm(place, gain, tokens, other_tokens, ids, other_ids):
    row_count, width = tokens.shape
    return pl.pallas_call(
        first_norm_kernel,
        out_shape=[
            jax.ShapeDtypeStruct((cores * row_count, width), jnp.bfloat16),
            jax.ShapeDtypeStruct((cores * row_count, width + lanes), jnp.bfloat16),
            jax.ShapeDtypeStruct(place.shape, place.dtype),
        ],
        in_specs=[in_vmem] * 6,
        out_specs=[in_vmem] * 3,
        compiler_params=pltpu.CompilerParams(vmem_limit_bytes=4 * 1024 * 1024),
    )(place, gain, tokens, other_tokens, ids, other_ids)


def hold_kernel(place_ref, *refs):
    count = (len(refs) - 2) // 2
    sources, place_out, targets, sems = refs[:count], refs[count], refs[count + 1 : -1], refs[-1]
    copies = [pltpu.make_async_copy(source, target, sems.at[i]) for i, (source, target) in enumerate(zip(sources, targets))]
    start_all(copies)
    place_out[...] = place_ref[...]
    wait_all(copies)


def hold(place, arrays):
    place, *held = pl.pallas_call(
        hold_kernel,
        out_shape=[jax.ShapeDtypeStruct(x.shape, x.dtype) for x in (place, *arrays)],
        in_specs=[in_vmem] + [in_hbm] * len(arrays),
        out_specs=[in_vmem] * (1 + len(arrays)),
        scratch_shapes=[pltpu.SemaphoreType.DMA((len(arrays),))],
        compiler_params=pltpu.CompilerParams(vmem_limit_bytes=1024 * 1024),
        cost_estimate=pl.CostEstimate(
            flops=0, bytes_accessed=2 * sum(x.size * x.dtype.itemsize for x in arrays), transcendentals=0
        ),
    )(place, *[hbm(x) for x in arrays])
    return place, held


def join_kernel(*refs):
    *refs, out_ref = refs
    rows = refs[0].shape[0]
    for i, ref in enumerate(refs):
        out_ref[i * rows : (i + 1) * rows, :] = ref[...]


def joined(blocks):
    rows, width = blocks[0].shape
    return pl.pallas_call(
        join_kernel,
        out_shape=jax.ShapeDtypeStruct((rows * len(blocks), width), jnp.bfloat16),
        in_specs=[in_vmem] * len(blocks),
        out_specs=in_vmem,
        compiler_params=pltpu.CompilerParams(vmem_limit_bytes=6 * 1024 * 1024),
    )(*blocks)


def expert_kernel(moment, micro_count, top_count, row_count, capacity, place_ref, *refs):
    *refs, router_ref, gate_ref, up_ref, down_ref, own_ref, other_ref, rows_ref, hidden_ref = refs
    count = len(refs) // 2
    rows_refs, ids_refs = refs[:count], refs[count:]
    inner_width, width = down_ref.shape
    inner_step, outer_step = 512, 512
    total_rows = rows_ref.shape[0]
    part_rows = total_rows // count
    expert_count = router_ref.shape[0]
    for i, ref in enumerate(rows_refs):
        rows_ref[i * part_rows : (i + 1) * part_rows, :] = ref[:, :width]

    owner, micro = owner_of(place_ref), micro_at(moment, micro_count, place_ref)
    ids = jnp.concatenate([ref[:, ref.shape[1] - lanes :].astype(jnp.float32) for ref in ids_refs], axis=0)
    names = lax.broadcasted_iota(jnp.int32, (total_rows, expert_count), 1).astype(jnp.float32)
    member = jnp.zeros((total_rows, expert_count), jnp.float32)
    for k in range(top_count):
        choice = ids[:, k : k + 1]
        for m in range(1, micro_count):
            at = m * top_count + k
            choice = jnp.where(micro == m, ids[:, at : at + 1], choice)
        member = jnp.where(choice == names, 1.0, member)
    mine = names == owner.astype(jnp.float32)
    row_at = lax.broadcasted_iota(jnp.int32, (total_rows, total_rows), 0)
    column_at = lax.broadcasted_iota(jnp.int32, (total_rows, total_rows), 1)
    before = (column_at < row_at) & (column_at // row_count == row_at // row_count)
    named = jnp.where(mine, member, 0.0)
    earlier = jnp.dot(
        jnp.where(before, 1.0, 0.0).astype(jnp.bfloat16), named.astype(jnp.bfloat16), preferred_element_type=jnp.float32
    )
    slot = jnp.sum(jnp.where(mine, earlier, 0.0), axis=1, keepdims=True)
    kept = (jnp.sum(named, axis=1, keepdims=True) > 0.5) & (slot < capacity - 0.5)
    logits = lax.dot_general(rows_ref[...], router_ref[...], (((1,), (1,)), ((), ())), preferred_element_type=jnp.float32)
    scores = jax.nn.sigmoid(logits)
    total = jnp.sum(jnp.where(member > 0.5, scores, 0.0), axis=1, keepdims=True)
    own = jnp.sum(jnp.where(mine, scores, 0.0), axis=1, keepdims=True)
    factor = jnp.where(kept, routed_scale * own / total, 0.0)

    for at in range(0, inner_width, inner_step):
        part = slice(at, at + inner_step)
        gate_part = jnp.dot(rows_ref[...], gate_ref[:, part], preferred_element_type=jnp.float32)
        up_part = jnp.dot(rows_ref[...], up_ref[:, part], preferred_element_type=jnp.float32)
        hidden = gate_part / (1.0 + jnp.exp(-gate_part)) * up_part
        hidden_ref[:, part] = jnp.where(kept, hidden * factor, 0.0).astype(jnp.bfloat16)
    hidden = hidden_ref[...]
    for at in range(0, width, outer_step):
        part = slice(at, at + outer_step)
        share = jnp.dot(hidden, down_ref[:, part], preferred_element_type=jnp.float32)
        own_ref[:, part] = share[: total_rows // cores]
        other_ref[:, part] = share[total_rows // cores :].astype(jnp.bfloat16)


def expert_shares(moment, micro_count, top_count, row_count, capacity, place, rows, ids, weights):
    part_rows = rows[0].shape[0]
    inner_width, width = weights[3].shape
    total_rows = len(rows) * part_rows
    return pl.pallas_call(
        functools.partial(expert_kernel, moment, micro_count, top_count, row_count, capacity),
        out_shape=[jax.ShapeDtypeStruct((total_rows // cores, width), kind) for kind in (jnp.float32, jnp.bfloat16)],
        in_specs=[in_vmem] * (1 + 2 * len(rows) + 4),
        out_specs=[in_vmem] * 2,
        scratch_shapes=[pltpu.VMEM((total_rows, width), jnp.bfloat16), pltpu.VMEM((total_rows, inner_width), jnp.bfloat16)],
        compiler_params=pltpu.CompilerParams(vmem_limit_bytes=10 * 1024 * 1024),
        cost_estimate=pl.CostEstimate(
            flops=6 * total_rows * width * inner_width, bytes_accessed=6 * width * inner_width, transcendentals=0
        ),
    )(place, *rows, *ids, *weights)


def spread_kernel(entering, place_ref, hidden_ref, own_ref, other_ref, *refs):
    rows = hidden_ref.shape[0]
    if entering is not None:
        tokens_ref, *refs = refs
    for i, out_ref in enumerate(refs[::-1]):
        part = slice(i * rows, (i + 1) * rows)
        block = own_ref[part, :] + other_ref[part, :].astype(jnp.float32)
        if i == 0:
            block = jnp.where(core_of(place_ref) == 0, block + hidden_ref[...].astype(jnp.float32), block)
            if entering is not None:
                block = jnp.where(section_of(place_ref) == entering, tokens_ref[...].astype(jnp.float32), block)
        out_ref[...] = block.astype(jnp.bfloat16)


def spread(entering, place, hidden, own, other, *tokens):
    count = own.shape[0] // hidden.shape[0]
    return pl.pallas_call(
        functools.partial(spread_kernel, entering),
        out_shape=[jax.ShapeDtypeStruct(hidden.shape, jnp.bfloat16)] * count,
        in_specs=[in_vmem] * (4 + len(tokens)),
        out_specs=[in_vmem] * count,
        compiler_params=pltpu.CompilerParams(vmem_limit_bytes=8 * 1024 * 1024),
    )(place, hidden, own, other, *tokens)


def partial_kernel(*refs):
    *refs, out_ref = refs
    total = refs[0][...].astype(jnp.float32)
    for ref in refs[1:]:
        total = total + ref[...].astype(jnp.float32)
    out_ref[...] = total.astype(jnp.bfloat16)


def partial_sum(parts):
    return pl.pallas_call(
        partial_kernel,
        out_shape=jax.ShapeDtypeStruct(parts[0].shape, jnp.bfloat16),
        in_specs=[in_vmem] * len(parts),
        out_specs=in_vmem,
        compiler_params=pltpu.CompilerParams(vmem_limit_bytes=4 * 1024 * 1024),
    )(*parts)


def both(one_ref, two_ref):
    return one_ref[...].astype(jnp.float32) + two_ref[...].astype(jnp.float32)


def land_kernel(place_ref, gain_ref, one_ref, two_ref, *refs):
    *waiting, hidden_ref, out_ref = refs
    hidden = both(one_ref, two_ref)
    if waiting:
        hidden = jnp.where(section_of(place_ref) == 0, waiting[0][...].astype(jnp.float32), hidden)
    hidden_ref[...] = hidden.astype(jnp.bfloat16)
    hidden = hidden.astype(jnp.bfloat16).astype(jnp.float32)
    out_ref[...] = normalize(hidden, gain_ref[...].astype(jnp.float32)).astype(jnp.bfloat16)


def land(place, gain, one, two, *waiting):
    return pl.pallas_call(
        land_kernel,
        out_shape=[jax.ShapeDtypeStruct(one.shape, jnp.bfloat16)] * 2,
        in_specs=[in_vmem] * (4 + len(waiting)),
        out_specs=[in_vmem] * 2,
        compiler_params=pltpu.CompilerParams(vmem_limit_bytes=4 * 1024 * 1024),
    )(place, gain, one, two, *waiting)


def finish_kernel(final, place_ref, one_ref, two_ref, *refs):
    *mixed, out_ref = refs
    row_count = out_ref.shape[0]
    result = both(one_ref, two_ref).astype(jnp.bfloat16).astype(jnp.float32)
    if mixed:
        result = jnp.where(section_of(place_ref) == final, result, mixed[0][...].astype(jnp.float32))
    result = jnp.where(core_of(place_ref) == 0, result[:row_count], result[row_count:])
    out_ref[...] = result.astype(jnp.bfloat16)


def finish(final, place, one, two, *mixed):
    rows, width = one.shape
    return pl.pallas_call(
        functools.partial(finish_kernel, final),
        out_shape=jax.ShapeDtypeStruct((rows // cores, width), jnp.bfloat16),
        in_specs=[in_vmem] * (3 + len(mixed)),
        out_specs=in_vmem,
        compiler_params=pltpu.CompilerParams(vmem_limit_bytes=4 * 1024 * 1024),
    )(place, one, two, *mixed)


def per_device(tokens, norm_gain, router, w_gate, w_up, w_down, expert_ids):
    sections = lax.axis_size("section")
    section_index = lax.axis_index("section")
    expert_count = lax.axis_size("expert")
    owner = lax.axis_index("expert")
    micro_count = expert_ids.shape[1]
    row_count = tokens.shape[1]
    width = tokens.shape[2]
    top_count = expert_ids.shape[3]
    capacity = min(row_count, max(2, 5 * row_count * top_count // (4 * expert_count)))
    router_rows = jnp.transpose(router[0])
    gate, up, down = (w[0, 0] for w in (w_gate, w_up, w_down))
    own_ids = expert_ids[0]
    inner = expert_count // outer_size
    swap = [(e, e + 1 - 2 * (e % cores)) for e in range(expert_count)]

    def swapped(rows):
        return lax.ppermute(rows, "expert", swap)

    places = inner // cores
    shifts = sorted(range(outer_size), key=lambda k: -min(k, outer_size - k))
    steps = [(j, k) for k in shifts for j in reversed(range(places // cores))]

    def sent(rows, route, step, sign, first_core=()):
        j, k = step
        pairs = []
        for a, b in (*route, *first_core):
            for e in range(expert_count):
                o, x, c = e // inner, e % inner // cores, e % cores
                o = (o + sign * k) % outer_size
                x = (x + sign * (c * (places // cores) + j)) % places
                if c == 0 or (a, b) in route:
                    pairs.append((a * expert_count + e, b * expert_count + o * inner + x * cores + c))
        return lax.ppermute(rows, ("section", "expert"), pairs)

    place = jnp.where(jnp.arange(lanes, dtype=jnp.int32)[None] == 0, owner, section_index).astype(jnp.int32)
    stay = [(s, s) for s in range(sections)]
    mixed = ids = None
    final = sections - 1
    total_moments = sections + micro_count - 1
    for moment in range(total_moments):
        if moment == 0:
            place, (own_tokens, gain, held_ids) = hold(place, (tokens[0], norm_gain, own_ids))
            incoming, normed, place = first_norm(
                place, gain, own_tokens, swapped(tokens[0]), held_ids, swapped(own_ids)
            )
            entering_rows = incoming
        rows = [sent(normed, stay, step, 1) for step in steps[::-1]]
        if moment == 0:
            place, weights = hold(place, (router_rows, gate, up, down))
            rows, place = lax.optimization_barrier((rows, place))
        rows = joined(rows)
        rows = [rows, swapped(rows)]
        ids = rows if ids is None else ids
        own, other = expert_shares(moment, micro_count, top_count, row_count, capacity, place, rows, ids, weights)

        entering, finished = moment + 1, moment - final
        last = finished == micro_count - 1
        joint = sections == 2 and entering == final
        parts = spread(
            final if joint else None, place, incoming, own, swapped(other), *([entering_rows] if joint else [])
        )

        def arrived(route, first_core=(), parts=parts):
            moved = [sent(part, route, step, -1, () if any(step) else first_core) for step, part in zip(steps, parts)]
            part = partial_sum(moved)
            return part, swapped(part)

        if last:
            mixed = finish(final, place, *arrived(stay), *([] if mixed is None else [mixed]))
            break
        route = [(s, s + 1) for s in range(sections - 1)]
        back = [(final, 0)]
        waiting = []
        if not joint and entering < micro_count:
            waiting = [sent(entering_rows, [], steps[-1], -1, [(entering, 0)])]
            waiting = [jnp.where(owner % cores == 0, waiting[0], swapped(waiting[0]))]
        if finished > 0:
            one, two = arrived([(final, finished)])
            mixed = jnp.where(section_index == finished, (one.astype(jnp.float32) + two.astype(jnp.float32)).astype(jnp.bfloat16), mixed)
        one, two = arrived(route + back if finished == 0 else route, back if joint else ())
        incoming, normed = land(place, gain, one, two, *waiting)
        if finished == 0:
            mixed = incoming
    return mixed[None]


def solution(mesh):
    placed = (
        P("section", "expert", None),
        P("section", None),
        P("section", None, None),
        P("section", "expert", None, None),
        P("section", "expert", None, None),
        P("section", "expert", None, None),
        P("section", None, "expert", None),
    )
    return jax.shard_map(
        per_device,
        mesh=mesh,
        in_specs=placed,
        out_specs=P("section", "expert", None),
        check_vma=False,
    )
```
